512 devices in a mesh: row: 16 (over x, y), col: 32 (over z, core).
Axes of the slice: x: 4, y: 4, z: 16, core: 2. Of those that a mesh axis runs over, the one named last changes fastest.
Arguments:
- block_tiles: bfloat16 [16, 640, 128, 128], P('row', 'col'), may hold values from -0.15811388 to 0.15811388
- block_rows: int32 [16, 640], P('row', 'col'), may hold values from 0 to 15, as said below
- block_cols: int32 [16, 640], P('row', 'col'), may hold values from 0 to 7, as said below
- counts: int32 [16, 32], P('row', 'col'), may hold values from 1 to 20, as said below
- start_basis: bfloat16 [32768, 256], P('col'), may hold values from -6 to 6
Outputs:
- image_out: bfloat16 [32768, 256], P(('row', 'col'))
- basis_out: bfloat16 [32768, 256], P(('col', 'row'))
The draws below stay inside these ranges and needn't reach their ends.
Inputs may be any that keep to these rules, and one draw needn't show every extreme that they name: `block_rows`: each entry lies in 0 to 15; within the 20 slots of one slab pair no pair of block row and block column repeats. `block_cols`: each entry lies in 0 to 7; see block_rows. `counts`: some slab pair has all 20 slots live in every draw.
All inputs are finite; a program needn't handle non-finite values.
Results may differ from the reference program's by a relative error of at most 0.025.
Values may be sent and summed in bfloat16 or wider, within the bound.
A program may use at most 64 MiB of HBM per device.

```python
import jax
import jax.numpy as jnp
from jax import lax

BLOCK = 128
RANK = 256
BRD = 16
BCD = 8
NB = 20
MROWS = 32768
NCOLS = 32768
N_ROW = 16
N_COL = 32


def pair_slots(key):
    subkeys = jax.random.split(jax.random.fold_in(key, 11), N_ROW * N_COL)
    orders = jax.vmap(lambda sub: jax.random.permutation(sub, BRD * BCD)[:NB])(subkeys)
    return orders.reshape(N_ROW, N_COL * NB).astype(jnp.int32)


def draw_block_rows(key, part):
    return (pair_slots(key) // BCD).astype(jnp.int32)


def draw_block_cols(key, part):
    return (pair_slots(key) % BCD).astype(jnp.int32)


def draw_counts(key, part):
    quarters = jax.random.randint(jax.random.fold_in(key, 3), (N_ROW * N_COL,), 1, 5)
    loads = jnp.maximum(NB * quarters // 4, 1)
    chosen = jax.random.randint(jax.random.fold_in(key, 5), (), 0, N_ROW * N_COL)
    loads = jnp.where(jnp.arange(N_ROW * N_COL) == chosen, NB, loads)
    return loads.reshape(N_ROW, N_COL).astype(jnp.int32)


def draw_block_tiles(key, part):
    base = (BLOCK * NB * N_COL // (2 * BRD)) ** (-0.5)
    shape = (N_ROW, N_COL * NB, BLOCK, BLOCK)
    slab = (jnp.arange(N_COL * NB) // NB).astype(jnp.float32)
    position = slab / max(N_COL - 1, 1) - 0.5
    ratio = 2.5
    values = jax.random.normal(jax.random.fold_in(key, 21), shape, jnp.float32)
    values = jnp.clip(values, -4.0, 4.0)
    scales = jnp.exp(jnp.log(ratio) * position)
    scales = scales / jnp.sqrt(jnp.mean(scales * scales))
    return (values * base * scales[None, :, None, None]).astype(jnp.bfloat16)


def block_scale(own_key, shape, cuts, smallest, largest):
    def one(axis_at, shards_of):
        steps = jax.random.uniform(jax.random.fold_in(jax.random.fold_in(own_key, 6), axis_at), (shards_of,), jnp.float32, smallest / len(cuts), largest / len(cuts))
        return jnp.repeat(jnp.exp(steps), shape[axis_at] // shards_of).reshape((-1,) + (1,) * (len(shape) - axis_at - 1))

    factor_of = one(*cuts[0])
    for cut in cuts[1:]:
        factor_of = factor_of * one(*cut)
    return factor_of


def centred(stream_key, shape, deviation, reach, cuts=(), kind=jnp.bfloat16):
    entries = jax.random.normal(stream_key, shape, jnp.float32) * deviation
    if len(cuts) > 0:
        entries = block_scale(stream_key, shape, cuts, -0.22, 0.18) * entries
    return jnp.clip(entries, min=-reach, max=reach).astype(kind)


def setup_inputs(seed: int = 0) -> dict:
    streams_of = jax.random.split(jax.random.key(seed), 6)
    return {
        "block_tiles": draw_block_tiles(jax.random.fold_in(streams_of[5], 71), 0),
        "block_rows": draw_block_rows(jax.random.fold_in(streams_of[5], 71), 0),
        "block_cols": draw_block_cols(jax.random.fold_in(streams_of[5], 71), 0),
        "counts": draw_counts(jax.random.fold_in(streams_of[5], 71), 0),
        "start_basis": centred(streams_of[4], (NCOLS, RANK), 1.0, 6.0, ((0, 32),)),
    }


def one_hot(indices, width):
    return (indices[..., None] == jnp.arange(width, dtype=jnp.int32)).astype(jnp.float32)

def round_half(value):
    return lax.optimization_barrier(value.astype(jnp.bfloat16)).astype(jnp.float32)

def forward(tiles_all, rows_all, cols_all, live_all, basis_slab):
    basis_parts = basis_slab.reshape(N_COL, BCD, BLOCK, RANK)
    column_ids = jnp.arange(N_COL, dtype=jnp.int32)[:, None]

    def per_row(packed):
        row_tiles, row_ids, col_ids, live_slots = packed
        gathered = basis_parts[column_ids, col_ids].astype(jnp.float32)
        products = jnp.einsum('cnij,cnjk->cnik', row_tiles.astype(jnp.float32), gathered)
        select = one_hot(row_ids, BRD) * live_slots[..., None]
        partial_value = jnp.einsum('cna,cnik->caik', select, products, precision=lax.Precision.HIGHEST)
        summed = lax.optimization_barrier(jnp.sum(round_half(partial_value), axis=0))
        return summed.reshape(BRD * BLOCK, RANK).astype(jnp.bfloat16)
    return lax.map(per_row, (tiles_all, rows_all, cols_all, live_all)).reshape(MROWS, RANK)

def backward(tiles_all, rows_all, cols_all, live_all, image_slab):
    image_parts = image_slab.reshape(N_ROW, BRD, BLOCK, RANK)
    row_numbers = jnp.arange(N_ROW, dtype=jnp.int32)[:, None]

    def per_col(packed):
        col_tiles, row_ids, col_ids, live_slots = packed
        gathered = image_parts[row_numbers, row_ids].astype(jnp.float32)
        products = jnp.einsum('rnij,rnik->rnjk', col_tiles.astype(jnp.float32), gathered)
        select = one_hot(col_ids, BCD) * live_slots[..., None]
        partial_value = jnp.einsum('rnb,rnjk->rbjk', select, products, precision=lax.Precision.HIGHEST)
        summed = lax.optimization_barrier(jnp.sum(round_half(partial_value), axis=0))
        return summed.reshape(BCD * BLOCK, RANK)
    swapped = (jnp.swapaxes(tiles_all, 0, 1), jnp.swapaxes(rows_all, 0, 1), jnp.swapaxes(cols_all, 0, 1), jnp.swapaxes(live_all, 0, 1))
    return lax.map(per_col, swapped).reshape(NCOLS, RANK)

def normalize(summed):
    mean_square = lax.optimization_barrier(jnp.mean(summed * summed, axis=0))
    return (summed / jnp.sqrt(mean_square + 1e-06)).astype(jnp.bfloat16)

def reference(block_tiles, block_rows, block_cols, counts, start_basis):
    tiles_all = block_tiles.reshape(N_ROW, N_COL, NB, BLOCK, BLOCK)
    rows_all = block_rows.reshape(N_ROW, N_COL, NB).astype(jnp.int32)
    cols_all = block_cols.reshape(N_ROW, N_COL, NB).astype(jnp.int32)
    live_all = (jnp.arange(NB, dtype=jnp.int32)[None, None, :] < counts[:, :, None]).astype(jnp.float32)
    image_first = forward(tiles_all, rows_all, cols_all, live_all, start_basis)
    basis_first = normalize(backward(tiles_all, rows_all, cols_all, live_all, image_first))
    image_out = forward(tiles_all, rows_all, cols_all, live_all, basis_first)
    basis_out = normalize(backward(tiles_all, rows_all, cols_all, live_all, image_out))
    return (image_out, basis_out)
```

```python
import functools

import jax
import jax.numpy as jnp
from jax import lax
from jax.experimental import pallas as pl
from jax.experimental.pallas import tpu as pltpu
from jax.sharding import PartitionSpec as P

BLOCK = 128
BRD = 16
BCD = 8
NB = 20
HALF = 128
TOTAL = 32768.0
F32 = jnp.float32
BF16 = jnp.bfloat16


def kernel(
    tab_ref, tabv_ref, tiles_ref, start_ref, image_ref, basis_ref,
    ptab, ptabv, tl_own, tl_in, dense, bas, rs_f, rs_b, yt, acc, zc, r1, s2, r2, zfin, nbuf, ex_i, ex_b,
    pre_send, pre_recv, loc_sem, zs, zr, xs, xr, ns, nr, es, er,
):
    row = lax.axis_index("row")
    col = lax.axis_index("col")
    x, y = row // 4, row % 4
    z, c = col // 2, col % 2
    sg = 1 - 2 * c

    def at(xx, yy, zz, cc):
        return (((xx + 4) % 4) * 4 + (yy + 4) % 4, ((zz + 16) % 16) * 2 + cc)

    def zat(d):
        return at(x, y, z + d, c)

    def remote(src, dst, ssem, rsem, dev):
        return pltpu.make_async_remote_copy(
            src_ref=src, dst_ref=dst, send_sem=ssem, recv_sem=rsem,
            device_id=dev, device_id_type=pl.DeviceIdType.MESH,
        )

    partner = at(x, y, z, 1 - c)

    def norm_peer(stage, k):
        if stage == 0:
            return at(x + k, y, z, c)
        if stage == 1:
            return at(x, y + k, z, c)
        if stage == 2:
            return at(x, y, (z // 4) * 4 + (z + k) % 4, c)
        return at(x, y, z + 4 * k, c)

    barrier = pltpu.get_barrier_semaphore()
    peers = [partner, zat(1), zat(-1)]
    peers += [norm_peer(st, k) for st in range(4) for k in (1, 2, 3)]
    for dev in peers:
        pl.semaphore_signal(barrier, inc=1, device_id=dev, device_id_type=pl.DeviceIdType.MESH)

    own_tiles = pltpu.make_async_copy(tiles_ref.at[0], tl_own.at[pl.ds(0, NB)], loc_sem.at[0])
    own_tiles.start()
    mine = pl.ds(pl.multiple_of(c * HALF, HALF), HALF)
    theirs = pl.ds(pl.multiple_of((1 - c) * HALF, HALF), HALF)
    own_start = pltpu.make_async_copy(start_ref.at[:, :, :, mine], bas.at[0, c], loc_sem.at[1])
    own_start.start()
    zero_tile = jnp.zeros((BLOCK, BLOCK), BF16)
    tl_own[NB] = zero_tile
    tl_in[NB] = zero_tile

    pl.semaphore_wait(barrier, len(peers))
    pre = [
        remote(tabv_ref, ptabv, pre_send.at[0], pre_recv.at[0], partner),
        remote(tiles_ref.at[0], tl_in.at[pl.ds(0, NB)], pre_send.at[1], pre_recv.at[1], partner),
        remote(start_ref.at[:, :, :, theirs], bas.at[0, c], pre_send.at[2], pre_recv.at[2], partner),
    ]
    for copy in pre:
        copy.start()

    def build(which, tl, table):
        def one_row(i, carry):
            for j in range(BCD):
                dense[which, i, :, j * BLOCK : (j + 1) * BLOCK] = tl[table[0, i * BCD + j]]
            return carry

        lax.fori_loop(0, BRD, one_row, 0)

    own_tiles.wait()
    build(c, tl_own, tab_ref)
    incoming = [
        remote(tabv_ref, ptabv, pre_send.at[0], pre_recv.at[0], partner),
        remote(tiles_ref.at[0], tl_in.at[pl.ds(0, NB)], pre_send.at[1], pre_recv.at[1], partner),
        remote(start_ref.at[:, :, :, theirs], bas.at[0, 1 - c], pre_send.at[2], pre_recv.at[2], partner),
    ]
    incoming[0].wait_recv()
    table_in = pltpu.make_async_copy(ptabv, ptab, loc_sem.at[2])
    table_in.start()
    table_in.wait()
    incoming[1].wait_recv()
    build(1 - c, tl_in, ptab)
    incoming[2].wait_recv()
    own_start.wait()
    for copy in pre:
        copy.wait_send()

    def product(it, d):
        d = (d + 32) % 16
        left = bas[it, 0].reshape(1024, HALF)
        right = bas[it, 1].reshape(1024, HALF)
        return jnp.dot(dense[0, d], left, preferred_element_type=F32) + jnp.dot(
            dense[1, d], right, preferred_element_type=F32
        )

    def z_fwd(it, s, src, dst, phase):
        return remote(src, dst, zs.at[it, phase, 0, s], zr.at[it, phase, 0, s], zat(sg))

    def z_bwd(it, s, src, dst, phase):
        return remote(src, dst, zs.at[it, phase, 1, s], zr.at[it, phase, 1, s], zat(-sg))

    def rs_send_f(it, s):
        src = rs_f.at[it, s]
        return z_fwd(it, s, src, rs_f.at[it, s + 1], 0)

    def rs_send_b(it, s):
        src = rs_b.at[it, s]
        return z_bwd(it, s, src, rs_b.at[it, s + 1], 0)

    def ag_send_f(it, s):
        piece = yt.at[it, (z - sg * s + 32) % 16]
        return z_fwd(it, s, piece, piece, 1)

    def ag_send_b(it, s):
        piece = yt.at[it, (z + sg * s + 32) % 16]
        return z_bwd(it, s, piece, piece, 1)

    def ag_recv_f(it, s):
        piece = yt.at[it, (z - sg * (s + 1) + 32) % 16]
        return z_fwd(it, s, piece, piece, 1)

    def ag_recv_b(it, s):
        piece = yt.at[it, (z + sg * (s + 1) + 32) % 16]
        return z_bwd(it, s, piece, piece, 1)

    def ring_dev(axis, d):
        if axis == 0:
            return at(x + d, y, z, c)
        return at(x, y + d, z, c)

    def coord(axis):
        return x if axis == 0 else y

    def xy_copy(it, phase, stage, h, way, msg, axis, src, dst):
        i = (it, phase, stage, h, way * 3 + msg)
        return remote(src, dst, xs.at[i], xr.at[i], ring_dev(axis, sg if way == 0 else -sg))

    def rs4_copies(it, stage, h, axis):
        buf = zc.at[it, h] if stage == 0 else s2.at[it, h]
        rb = r1.at[it, h] if stage == 0 else r2.at[it, h]
        a = coord(axis)
        far = (a + 2) % 4
        nxt = (a + sg + 4) % 4
        prv = (a - sg + 4) % 4
        plan = [(0, 0, far, 0), (1, 0, far, 1), (0, 1, nxt, 1), (1, 1, prv, 0), (0, 2, nxt, 0), (1, 2, prv, 1)]
        return {
            (way, msg): xy_copy(it, 0, stage, h, way, msg, axis, buf.at[g, sub], rb.at[way * 3 + msg])
            for way, msg, g, sub in plan
        }

    def rs4(it, stage, axes):
        copies = [rs4_copies(it, stage, h, axes[h]) for h in (0, 1)]
        for key in ((0, 0), (1, 0), (0, 1), (1, 1)):
            for h in (0, 1):
                copies[h][key].start()
        for way in (0, 1):
            for h in (0, 1):
                buf, rb = (zc, r1) if stage == 0 else (s2, r2)
                a = coord(axes[h])
                g = (a + sg + 4) % 4 if way == 0 else (a - sg + 4) % 4
                copies[h][way, 0].wait_recv()
                total = buf[it, h, g, way].astype(F32) + rb[it, h, way * 3].astype(F32)
                buf[it, h, g, way] = total.astype(BF16)
                copies[h][way, 2].start()
        result = []
        for h in (0, 1):
            buf, rb = (zc, r1) if stage == 0 else (s2, r2)
            a = coord(axes[h])
            for key in ((0, 1), (1, 1), (0, 2), (1, 2)):
                copies[h][key].wait_recv()
            low = buf[it, h, a, 0].astype(F32) + rb[it, h, 2].astype(F32) + rb[it, h, 4].astype(F32)
            high = buf[it, h, a, 1].astype(F32) + rb[it, h, 1].astype(F32) + rb[it, h, 5].astype(F32)
            result.append((low, high))
        return result, copies

    def piece_ref(it, h, stage, axis, g, sub):
        if stage == 0:
            rows = pl.ds(sub * 32, 32)
            if axis == 0:
                return bas.at[it, h, g, y, rows]
            return bas.at[it, h, x, g, rows]
        pair = pl.ds(sub * 2, 2)
        if axis == 0:
            return bas.at[it, h, g, pair]
        return bas.at[it, h, pair, g]

    def ag4_copies(it, stage, h, axis):
        a = coord(axis)
        nxt = (a + sg + 4) % 4
        prv = (a - sg + 4) % 4
        plan = [(0, 0, a, 0), (1, 0, a, 1), (0, 1, a, 1), (1, 1, a, 0), (0, 2, prv, 0), (1, 2, nxt, 1)]
        out = {}
        for way, msg, g, sub in plan:
            ref = piece_ref(it, h, stage, axis, g, sub)
            out[way, msg] = xy_copy(it, 1, stage, h, way, msg, axis, ref, ref)
        return out

    def ag4_recv(it, stage, h, axis, way, msg):
        a = coord(axis)
        nxt = (a + sg + 4) % 4
        prv = (a - sg + 4) % 4
        far = (a + 2) % 4
        g, sub = {
            (0, 0): (prv, 0), (1, 0): (nxt, 1), (0, 1): (prv, 1),
            (1, 1): (nxt, 0), (0, 2): (far, 0), (1, 2): (far, 1),
        }[way, msg]
        ref = piece_ref(it, h, stage, axis, g, sub)
        xy_copy(it, 1, stage, h, way, msg, axis, ref, ref).wait_recv()

    def ag4_start(it, stage, axes):
        copies = [ag4_copies(it, stage, h, axes[h]) for h in (0, 1)]
        for key in ((0, 0), (1, 0), (0, 1), (1, 1)):
            for h in (0, 1):
                copies[h][key].start()
        return copies

    def ag4_finish(it, stage, axes, copies):
        for way in (0, 1):
            for h in (0, 1):
                ag4_recv(it, stage, h, axes[h], way, 0)
                copies[h][way, 2].start()
        for key in ((0, 1), (1, 1), (0, 2), (1, 2)):
            for h in (0, 1):
                ag4_recv(it, stage, h, axes[h], *key)

    def norm_copy(it, stage, k):
        return remote(
            nbuf.at[it, stage, 0], nbuf.at[it, stage, k], ns.at[it, stage, k], nr.at[it, stage, k],
            norm_peer(stage, k),
        )

    def norm_start(it, stage, value):
        nbuf[it, stage, 0] = jnp.broadcast_to(value, (8, HALF))
        for k in (1, 2, 3):
            norm_copy(it, stage, k).start()

    def norm_finish(it, stage):
        for k in (1, 2, 3):
            norm_copy(it, stage, k).wait_recv()
        return (nbuf[it, stage, 0] + nbuf[it, stage, 1] + nbuf[it, stage, 2] + nbuf[it, stage, 3])[0:1]

    def scale_of(total):
        return lax.rsqrt(total / TOTAL + 1e-06)

    def add_products(it, pieces, first):
        for which in (0, 1):
            for part in range(2):
                cols = pl.ds(part * 512, 512)
                total = None if first else acc[which, :, cols]
                for p in pieces:
                    term = jnp.dot(yt[it, p], dense[which, p, :, cols], preferred_element_type=F32)
                    total = term if total is None else total + term
                acc[which, :, cols] = total

    lane = lax.broadcasted_iota(jnp.int32, (HALF, BLOCK), 1) < 64

    for it in (0, 1):
        rs_f[it, 0] = product(it, z + sg * 8).astype(BF16)
        rs_send_f(it, 0).start()
        rs_b[it, 0] = product(it, z - sg * 7).astype(BF16)
        rs_send_b(it, 0).start()
        if it == 1:
            norm_start(0, 2, norm_finish(0, 1))

        def rs_step(s, carry):
            ahead = product(it, z + sg * (8 - s))
            behind = product(it, z - sg * (7 - s))
            rs_send_f(it, s - 1).wait_recv()
            rs_f[it, s] = (ahead + rs_f[it, s].astype(F32)).astype(BF16)
            rs_send_f(it, s).start()
            rs_send_b(it, s - 1).wait_recv()
            rs_b[it, s] = (behind + rs_b[it, s].astype(F32)).astype(BF16)
            rs_send_b(it, s).start()
            return carry

        if it == 0:
            lax.fori_loop(1, 7, rs_step, 0)
        else:
            lax.fori_loop(1, 4, rs_step, 0)
            norm_start(0, 3, norm_finish(0, 2))
            lax.fori_loop(4, 7, rs_step, 0)
        ahead = product(it, z + sg)
        own = product(it, z)
        rs_send_f(it, 6).wait_recv()
        rs_f[it, 7] = (ahead + rs_f[it, 7].astype(F32)).astype(BF16)
        rs_send_f(it, 7).start()
        rs_send_b(it, 6).wait_recv()
        own = own + rs_b[it, 7].astype(F32)
        if it == 1:
            scale = scale_of(norm_finish(0, 3))
        rs_send_f(it, 7).wait_recv()
        own = own + rs_f[it, 8].astype(F32)
        if it == 1:
            own = own * scale
        own = own.astype(BF16)

        yt[it, z] = own.astype(F32).T.astype(BF16)
        ag_send_f(it, 0).start()
        ag_send_b(it, 0).start()
        if it == 1:
            ex_i[0] = own[:64]
            ex_i[1] = own[64:]
            swap_i = remote(ex_i.at[1 - c], ex_i.at[2], es.at[0], er.at[0], partner)
            swap_i.start()
        add_products(it, [z], True)

        def ag_step(s, carry):
            ag_recv_f(it, s).wait_recv()
            ag_send_f(it, s + 1).start()
            ag_recv_b(it, s).wait_recv()

            @pl.when(s < 6)
            def _():
                ag_send_b(it, s + 1).start()

            add_products(it, [(z - sg * (s + 1) + 32) % 16, (z + sg * (s + 1) + 32) % 16], False)
            return carry

        lax.fori_loop(0, 7, ag_step, 0)
        if it == 1:
            swap_i.wait()
            image_ref[:, mine] = ex_i[c]
            image_ref[:, theirs] = ex_i[2]
        ag_recv_f(it, 7).wait_recv()
        add_products(it, [(z + 8) % 16], False)

        for j in range(BCD):
            blk = slice(j * BLOCK, (j + 1) * BLOCK)
            zero_half = acc[0, :, blk]
            one_half = acc[1, :, blk]
            pair = (
                jnp.where(lane, zero_half, pltpu.roll(one_half, 64, 1)).astype(BF16),
                jnp.where(lane, pltpu.roll(zero_half, 64, 1), one_half).astype(BF16),
            )
            for odd in (0, 1):
                xx, yy = divmod(2 * j + odd, 4)
                zc[it, 0, xx, yy // 2, yy % 2] = pair[odd][:64]
                zc[it, 1, yy, xx // 2, xx % 2] = pair[odd][64:]
        first, copies_a = rs4(it, 0, (0, 1))
        for h in (0, 1):
            for pos in range(4):
                value = first[h][pos // 2][pos % 2].astype(BF16)
                s2[it, h, pos, 0] = value[:32]
                s2[it, h, pos, 1] = value[32:]
        second, copies_b = rs4(it, 1, (1, 0))
        ranks = jnp.concatenate([second[0][0], second[0][1], second[1][0], second[1][1]], axis=0)
        rows = ranks.T
        squares = jnp.sum(rows * rows, axis=0, keepdims=True)
        if it == 0:
            low = rows.astype(BF16)
            bas[1, 0, x, y] = low[:64]
            bas[1, 1, x, y] = low[64:]
            copies_c = ag4_start(1, 0, (1, 0))
            norm_start(0, 0, squares)
            ag4_finish(1, 0, (1, 0), copies_c)
            copies_d = ag4_start(1, 1, (0, 1))
            norm_start(0, 1, norm_finish(0, 0))
            ag4_finish(1, 1, (0, 1), copies_d)
            for copies in copies_c + copies_d:
                for copy in copies.values():
                    copy.wait_send()
        else:
            norm_start(1, 0, squares)
            zfin[...] = rows
            norm_start(1, 1, norm_finish(1, 0))
            norm_start(1, 2, norm_finish(1, 1))
            norm_start(1, 3, norm_finish(1, 2))
            scale = scale_of(norm_finish(1, 3))
            low = (zfin[...] * scale).astype(BF16)
            ex_b[0] = low[:64]
            ex_b[1] = low[64:]
            swap_b = remote(ex_b.at[1 - c], ex_b.at[2], es.at[1], er.at[1], partner)
            swap_b.start()
            basis_ref[:, mine] = ex_b[c]
            swap_b.wait()
            basis_ref[:, theirs] = ex_b[2]
        for copies in copies_a + copies_b:
            for copy in copies.values():
                copy.wait_send()

    for it in (0, 1):

        def drain(s, carry):
            rs_send_f(it, s).wait_send()
            rs_send_b(it, s).wait_send()
            ag_send_f(it, s).wait_send()
            ag_send_b(it, s).wait_send()
            return carry

        lax.fori_loop(0, 7, drain, 0)
        rs_send_f(it, 7).wait_send()
        ag_send_f(it, 7).wait_send()
        for stage in range(4):
            for k in (1, 2, 3):
                norm_copy(it, stage, k).wait_send()


def shards(block_tiles, block_rows, block_cols, counts, start_basis):
    slots = jnp.arange(NB, dtype=jnp.int32)
    place = jnp.where(slots < counts[0, 0], block_rows[0] * BCD + block_cols[0], -1)
    hit = place[None, :] == jnp.arange(BRD * BCD, dtype=jnp.int32)[:, None]
    table = NB + jnp.sum(jnp.where(hit, slots[None, :] - NB, 0), axis=1, dtype=jnp.int32)
    table = table[None, :]
    start = start_basis.reshape(4, 4, 64, 2 * HALF)
    dma = pltpu.SemaphoreType.DMA
    vmem = pltpu.VMEM
    scratch = [
        pltpu.SMEM((1, 128), jnp.int32),
        vmem((1, 128), jnp.int32),
        vmem((NB + 1, BLOCK, BLOCK), BF16),
        vmem((NB + 1, BLOCK, BLOCK), BF16),
        vmem((2, BRD, BLOCK, 1024), BF16),
        vmem((2, 2, 4, 4, 64, HALF), BF16),
        vmem((2, 9, BLOCK, HALF), BF16),
        vmem((2, 8, BLOCK, HALF), BF16),
        vmem((2, 16, HALF, BLOCK), BF16),
        vmem((2, HALF, 1024), F32),
        vmem((2, 2, 4, 2, 2, 64, BLOCK), BF16),
        vmem((2, 2, 6, 2, 64, BLOCK), BF16),
        vmem((2, 2, 4, 2, 32, BLOCK), BF16),
        vmem((2, 2, 6, 32, BLOCK), BF16),
        vmem((BLOCK, HALF), F32),
        vmem((2, 4, 4, 8, HALF), F32),
        vmem((3, 64, HALF), BF16),
        vmem((3, 64, HALF), BF16),
        dma((3,)), dma((3,)), dma((3,)),
        dma((2, 2, 2, 8)), dma((2, 2, 2, 8)),
        dma((2, 2, 2, 2, 6)), dma((2, 2, 2, 2, 6)),
        dma((2, 4, 4)), dma((2, 4, 4)),
        dma((2,)), dma((2,)),
    ]
    anywhere = pl.BlockSpec(memory_space=pl.ANY)
    in_vmem = pl.BlockSpec(memory_space=pltpu.VMEM)
    return pl.pallas_call(
        kernel,
        out_shape=(
            jax.ShapeDtypeStruct((64, 2 * HALF), BF16),
            jax.ShapeDtypeStruct((64, 2 * HALF), BF16),
        ),
        in_specs=[pl.BlockSpec(memory_space=pltpu.SMEM), in_vmem, anywhere, anywhere],
        out_specs=(in_vmem, in_vmem),
        scratch_shapes=scratch,
        compiler_params=pltpu.CompilerParams(
            collective_id=0, has_side_effects=True, vmem_limit_bytes=48 * 1024 * 1024
        ),
    )(table, table, block_tiles, start)


def solution(mesh):
    in_specs = (
        P("row", "col", None, None), P("row", "col"), P("row", "col"), P("row", "col"), P("col", None),
    )
    out_specs = (P(("row", "col"), None), P(("col", "row"), None))
    return jax.shard_map(shards, mesh=mesh, in_specs=in_specs, out_specs=out_specs, check_vma=False)
```

```python
import functools

import jax
import jax.numpy as jnp
from jax import lax
from jax.experimental import pallas as pl
from jax.experimental.pallas import tpu as pltpu
from jax.sharding import PartitionSpec as P

BLOCK = 128
BRD = 16
BCD = 8
NB = 20
HALF = 128
TOTAL = 32768.0
F32 = jnp.float32
BF16 = jnp.bfloat16


TO_AGGREGATOR = ((8, 3), (7, 2), (-7, -2), (3, -2), (-3, 2), (6, 1), (-6, -1), (4, -1), (-4, 1))
TO_OWNER = ((5, 5), (-5, -5), (2, 2), (-2, -2), (1, 1), (-1, -1))
RELAYED = ((3, 3), (2, 2), (-2, -2), (1, 1), (-1, -1))


def kernel(
    rows_ref, cols_ref, counts_ref, tiles_ref, start_ref, image_ref, basis_ref,
    srows, scols, scount, tab, ptab, tabv, ptabv, tl_own, tl_in, dense, bas, zsnd, zrcv, yt, acc,
    zc, r1, s2, r2, zfin, nbuf, ex_i, ex_b,
    pre_send, pre_recv, loc_sem, zs, zr, xs, xr, ns, nr, es, er,
):
    row = lax.axis_index("row")
    col = lax.axis_index("col")
    x, y = row // 4, row % 4
    z, c = col // 2, col % 2
    sg = 1 - 2 * c

    def at(xx, yy, zz, cc):
        return (((xx + 4) % 4) * 4 + (yy + 4) % 4, ((zz + 16) % 16) * 2 + cc)

    def zpos(e):
        return (z + sg * e + 16) % 16

    def zdev(e):
        return (row, zpos(e) * 2 + c)

    def remote(src, dst, ssem, rsem, dev):
        return pltpu.make_async_remote_copy(
            src_ref=src, dst_ref=dst, send_sem=ssem, recv_sem=rsem,
            device_id=dev, device_id_type=pl.DeviceIdType.MESH,
        )

    partner = (row, z * 2 + 1 - c)
    pending = []

    def norm_dev(stage, k):
        if stage == 0:
            return ((row + k) % 16, col)
        return (row, ((z + k) % 16) * 2 + c)

    barrier = pltpu.get_barrier_semaphore()

    def greet(dev):
        pl.semaphore_signal(barrier, inc=1, device_id=dev, device_id_type=pl.DeviceIdType.MESH)

    greet(partner)

    def greet_line(k, carry):
        greet(norm_dev(1, k))
        greet(norm_dev(0, k))
        return carry

    lax.fori_loop(1, 16, greet_line, 0)

    local = [
        pltpu.make_async_copy(rows_ref, srows, loc_sem.at[0]),
        pltpu.make_async_copy(cols_ref, scols, loc_sem.at[1]),
        pltpu.make_async_copy(counts_ref, scount, loc_sem.at[2]),
        pltpu.make_async_copy(tiles_ref.at[0], tl_own.at[pl.ds(0, NB)], loc_sem.at[3]),
    ]
    for copy in local:
        copy.start()
    mine = pl.ds(pl.multiple_of(c * HALF, HALF), HALF)
    theirs = pl.ds(pl.multiple_of((1 - c) * HALF, HALF), HALF)
    own_start = pltpu.make_async_copy(start_ref.at[:, :, :, mine], bas.at[0, c], loc_sem.at[4])
    own_start.start()
    zero_tile = jnp.zeros((BLOCK, BLOCK), BF16)
    tl_own[NB] = zero_tile
    tl_in[NB] = zero_tile

    for copy in local[:3]:
        copy.wait()
    places = lax.broadcasted_iota(jnp.int32, (1, BRD * BCD), 1)
    slot_of = jnp.full((1, BRD * BCD), NB, jnp.int32)
    for slot in range(NB):
        place = jnp.where(slot < scount[0, 0], srows[0, slot] * BCD + scols[0, slot], -1)
        slot_of = jnp.where(places == place, slot, slot_of)
    tabv[...] = slot_of
    table_own = pltpu.make_async_copy(tabv, tab, loc_sem.at[5])
    table_own.start()

    pl.semaphore_wait(barrier, 31)
    pre = [
        remote(tabv, ptabv, pre_send.at[0], pre_recv.at[0], partner),
        remote(tiles_ref.at[0], tl_in.at[pl.ds(0, NB)], pre_send.at[1], pre_recv.at[1], partner),
        remote(start_ref.at[:, :, :, theirs], bas.at[0, c], pre_send.at[2], pre_recv.at[2], partner),
    ]
    for copy in pre:
        copy.start()

    def build(which, tl, table):
        def one_row(i, carry):
            for j in range(BCD):
                dense[which, i, :, j * BLOCK : (j + 1) * BLOCK] = tl[table[0, i * BCD + j]]
            return carry

        lax.fori_loop(0, BRD, one_row, 0)

    table_own.wait()
    local[3].wait()
    build(c, tl_own, tab)
    pre[0].wait_recv()
    table_in = pltpu.make_async_copy(ptabv, ptab, loc_sem.at[6])
    table_in.start()
    table_in.wait()
    pre[1].wait_recv()
    build(1 - c, tl_in, ptab)
    remote(start_ref.at[:, :, :, theirs], bas.at[0, 1 - c], pre_send.at[2], pre_recv.at[2], partner).wait_recv()
    own_start.wait()
    for copy in pre:
        copy.wait_send()

    def product(it, d):
        left = bas[it, 0].reshape(1024, HALF)
        right = bas[it, 1].reshape(1024, HALF)
        return jnp.dot(dense[0, d], left, preferred_element_type=F32) + jnp.dot(
            dense[1, d], right, preferred_element_type=F32
        )

    def rs_copy(it, m, e):
        return remote(zsnd.at[it, m], zrcv.at[it, m], zs.at[it, 0, m], zr.at[it, 0, m], zdev(e))

    def rs_launch(it, m, owner, e):
        zsnd[it, m] = product(it, zpos(owner)).astype(BF16)
        rs_copy(it, m, e).start()

    def rs_arrived(it, m):
        rs_copy(it, m, 1).wait_recv()
        return zrcv[it, m].astype(F32)

    def z_reduce(it, late):
        rs_launch(it, 0, 8, 3)

        def outer(k, carry):
            m = 1 + 4 * k
            rs_launch(it, m, 7 - k, 2 - k)
            rs_launch(it, m + 1, k - 7, k - 2)
            rs_launch(it, m + 2, 3 + k, k - 2)
            rs_launch(it, m + 3, -3 - k, 2 - k)
            return carry

        lax.fori_loop(0, 2, outer, 0)
        ahead = product(it, zpos(5))
        behind = product(it, zpos(-5))
        late()
        for m in (0, 1, 3, 5, 7):
            ahead = ahead + rs_arrived(it, m)
        zsnd[it, 9] = ahead.astype(BF16)
        rs_copy(it, 9, 5).start()
        for m in (2, 4, 6, 8):
            behind = behind + rs_arrived(it, m)
        zsnd[it, 10] = behind.astype(BF16)
        rs_copy(it, 10, -5).start()

        def near(k, carry):
            m = 11 + 2 * k
            rs_launch(it, m, 2 - k, 2 - k)
            rs_launch(it, m + 1, k - 2, k - 2)
            return carry

        lax.fori_loop(0, 2, near, 0)
        own = product(it, z)
        for m in (11, 12, 13, 14, 9, 10):
            own = own + rs_arrived(it, m)
        return own

    def z_drain(it, phase):
        def drain(m, carry):
            piece = zsnd.at[it, 0] if phase == 0 else yt.at[it, 0]
            remote(piece, piece, zs.at[it, phase, m], zr.at[it, phase, m], zdev(1)).wait_send()
            return carry

        lax.fori_loop(0, 15, drain, 0)

    def ag_copy(it, m, owner, e):
        piece = yt.at[it, zpos(owner)]
        return remote(piece, piece, zs.at[it, 1, m], zr.at[it, 1, m], zdev(e))

    def add_products(it, pieces, first):
        for which in (0, 1):
            for part in range(2):
                cols = pl.ds(part * 512, 512)
                total = None if first else acc[which, :, cols]
                for e in pieces:
                    p = zpos(e)
                    term = jnp.dot(yt[it, p], dense[which, p, :, cols], preferred_element_type=F32)
                    total = term if total is None else total + term
                acc[which, :, cols] = total

    def z_gather(it, late):
        for m, (_, e) in enumerate(TO_OWNER):
            ag_copy(it, m, 0, e).start()
        late()
        add_products(it, [0], True)
        ag_copy(it, 0, -5, 1).wait_recv()
        for i, (_, e) in enumerate(RELAYED):
            ag_copy(it, 6 + i, -5, e).start()
        ag_copy(it, 1, 5, 1).wait_recv()
        for i, (_, e) in enumerate(RELAYED[1:]):
            ag_copy(it, 11 + i, 5, e).start()
        for m, e in ((2, -2), (3, 2), (4, -1), (5, 1)):
            ag_copy(it, m, e, 1).wait_recv()
        add_products(it, [-5, 5, -2, 2, -1, 1], False)
        for m, e in ((9, -6), (10, -4), (13, 4), (14, 6)):
            ag_copy(it, m, e, 1).wait_recv()
        add_products(it, [-6, -4, 4, 6], False)
        for m, e in ((7, -7), (8, -3), (11, 3), (12, 7), (6, -8)):
            ag_copy(it, m, e, 1).wait_recv()
        add_products(it, [-7, -3, 3, 7, -8], False)

    def coord(axis):
        return x if axis == 0 else y

    def axis_dev(axis, k):
        if axis == 0:
            return at(x + k, y, z, c)
        return at(x, y + k, z, c)

    def xy_copy(it, phase, stage, h, k, axis, src, dst):
        i = (it, phase, stage, h, k - 1)
        return remote(src, dst, xs.at[i], xr.at[i], axis_dev(axis, k))

    def xy_reduce(it, stage, axes, buf, landing):
        copies = []
        for k in (2, 1, 3):
            for h in (0, 1):
                group = (coord(axes[h]) + k) % 4
                copy = xy_copy(it, 0, stage, h, k, axes[h], buf.at[it, h, group], landing.at[it, h, k - 1])
                copy.start()
                copies.append(copy)
        totals = [buf[it, h, coord(axes[h])].astype(F32) for h in (0, 1)]
        for i, copy in enumerate(copies):
            h, k = i % 2, (2, 1, 3)[i // 2]
            copy.wait_recv()
            totals[h] = totals[h] + landing[it, h, k - 1].astype(F32)
        pending.extend(copy.wait_send for copy in copies)
        return totals

    def piece_ref(it, h, stage, axis, g):
        if stage == 0:
            return bas.at[it, h, g, y] if axis == 0 else bas.at[it, h, x, g]
        return bas.at[it, h, g] if axis == 0 else bas.at[it, h, :, g]

    def xy_gather_start(it, stage, axes):
        copies = []
        for k in (2, 1, 3):
            for h in (0, 1):
                ref = piece_ref(it, h, stage, axes[h], coord(axes[h]))
                copy = xy_copy(it, 1, stage, h, k, axes[h], ref, ref)
                copy.start()
                copies.append(copy)
        pending.extend(copy.wait_send for copy in copies)

    def xy_gather_finish(it, stage, axes):
        for k in (1, 3, 2):
            for h in (0, 1):
                ref = piece_ref(it, h, stage, axes[h], (coord(axes[h]) + 4 - k) % 4)
                xy_copy(it, 1, stage, h, k, axes[h], ref, ref).wait_recv()

    def norm_copy(it, stage, k):
        return remote(
            nbuf.at[it, stage, 0], nbuf.at[it, stage, k], ns.at[it, stage, k], nr.at[it, stage, k],
            norm_dev(stage, k),
        )

    def norm_start(it, stage, value):
        nbuf[it, stage, 0] = jnp.broadcast_to(value, (8, HALF))

        def one(k, carry):
            norm_copy(it, stage, k).start()
            return carry

        lax.fori_loop(1, 16, one, 0)

        def drain_all():
            def drain(k, carry):
                norm_copy(it, stage, k).wait_send()
                return carry

            lax.fori_loop(1, 16, drain, 0)

        pending.append(drain_all)

    def norm_finish(it, stage):
        def one(k, carry):
            norm_copy(it, stage, k).wait_recv()
            return carry

        lax.fori_loop(1, 16, one, 0)
        return jnp.sum(nbuf[it, stage], axis=0)[0:1]

    def scale_of(total):
        return lax.rsqrt(total / TOTAL + 1e-06)

    lane = lax.broadcasted_iota(jnp.int32, (HALF, BLOCK), 1) < 64

    for it in (0, 1):
        def share_norm():
            if it == 1:
                norm_start(0, 1, norm_finish(0, 0))

        own = z_reduce(it, share_norm)
        pending.append(functools.partial(z_drain, it, 0))
        if it == 1:
            own = own * scale_of(norm_finish(0, 1))
        own = own.astype(BF16)

        yt[it, z] = own.astype(F32).T.astype(BF16)

        def share_image():
            if it == 1:
                ex_i[0] = own[:64]
                ex_i[1] = own[64:]
                remote(ex_i.at[1 - c], ex_i.at[2], es.at[0], er.at[0], partner).start()

        z_gather(it, share_image)
        pending.append(functools.partial(z_drain, it, 1))
        for j in range(BCD):
            blk = slice(j * BLOCK, (j + 1) * BLOCK)
            zero_half = acc[0, :, blk]
            one_half = acc[1, :, blk]
            pair = (
                jnp.where(lane, zero_half, pltpu.roll(one_half, 64, 1)).astype(BF16),
                jnp.where(lane, pltpu.roll(zero_half, 64, 1), one_half).astype(BF16),
            )
            for odd in (0, 1):
                xx, yy = divmod(2 * j + odd, 4)
                zc[it, 0, xx, yy] = pair[odd][:64]
                zc[it, 1, yy, xx] = pair[odd][64:]
        first = xy_reduce(it, 0, (0, 1), zc, r1)
        for h in (0, 1):
            s2[it, h] = first[h].astype(BF16)
        second = xy_reduce(it, 1, (1, 0), s2, r2)
        rows = jnp.concatenate(second, axis=0).T
        squares = jnp.sum(rows * rows, axis=0, keepdims=True)
        if it == 0:
            low = rows.astype(BF16)
            bas[1, 0, x, y] = low[:64]
            bas[1, 1, x, y] = low[64:]
            xy_gather_start(1, 0, (1, 0))
            norm_start(0, 0, squares)
            xy_gather_finish(1, 0, (1, 0))
            xy_gather_start(1, 1, (0, 1))
            xy_gather_finish(1, 1, (0, 1))
        else:
            norm_start(1, 0, squares)
            zfin[...] = rows
            remote(ex_i.at[1 - c], ex_i.at[2], es.at[0], er.at[0], partner).wait()
            image_ref[:, mine] = ex_i[c]
            image_ref[:, theirs] = ex_i[2]
            norm_start(1, 1, norm_finish(1, 0))
            low = (zfin[...] * scale_of(norm_finish(1, 1))).astype(BF16)
            ex_b[0] = low[:64]
            ex_b[1] = low[64:]
            swap = remote(ex_b.at[1 - c], ex_b.at[2], es.at[1], er.at[1], partner)
            swap.start()
            basis_ref[:, mine] = ex_b[c]
            swap.wait()
            basis_ref[:, theirs] = ex_b[2]

    for drain in pending:
        drain()


def shards(block_tiles, block_rows, block_cols, counts, start_basis):
    start = start_basis.reshape(4, 4, 64, 2 * HALF)
    dma = pltpu.SemaphoreType.DMA
    vmem = pltpu.VMEM
    smem = pltpu.SMEM
    scratch = [
        smem((1, NB), jnp.int32), smem((1, NB), jnp.int32), smem((1, 1), jnp.int32),
        smem((1, 128), jnp.int32), smem((1, 128), jnp.int32),
        vmem((1, 128), jnp.int32), vmem((1, 128), jnp.int32),
        vmem((NB + 1, BLOCK, BLOCK), BF16),
        vmem((NB + 1, BLOCK, BLOCK), BF16),
        vmem((2, BRD, BLOCK, 1024), BF16),
        vmem((2, 2, 4, 4, 64, HALF), BF16),
        vmem((2, 15, BLOCK, HALF), BF16),
        vmem((2, 15, BLOCK, HALF), BF16),
        vmem((2, 16, HALF, BLOCK), BF16),
        vmem((2, HALF, 1024), F32),
        vmem((2, 2, 4, 4, 64, BLOCK), BF16),
        vmem((2, 2, 3, 4, 64, BLOCK), BF16),
        vmem((2, 2, 4, 64, BLOCK), BF16),
        vmem((2, 2, 3, 64, BLOCK), BF16),
        vmem((BLOCK, HALF), F32),
        vmem((2, 2, 16, 8, HALF), F32),
        vmem((3, 64, HALF), BF16),
        vmem((3, 64, HALF), BF16),
        dma((3,)), dma((3,)), dma((7,)),
        dma((2, 2, 15)), dma((2, 2, 15)),
        dma((2, 2, 2, 2, 3)), dma((2, 2, 2, 2, 3)),
        dma((2, 2, 16)), dma((2, 2, 16)),
        dma((2,)), dma((2,)),
    ]
    anywhere = pl.BlockSpec(memory_space=pl.ANY)
    in_vmem = pl.BlockSpec(memory_space=pltpu.VMEM)
    return pl.pallas_call(
        kernel,
        out_shape=(
            jax.ShapeDtypeStruct((64, 2 * HALF), BF16),
            jax.ShapeDtypeStruct((64, 2 * HALF), BF16),
        ),
        in_specs=[anywhere] * 5,
        out_specs=(in_vmem, in_vmem),
        scratch_shapes=scratch,
        compiler_params=pltpu.CompilerParams(
            collective_id=0, has_side_effects=True, vmem_limit_bytes=48 * 1024 * 1024
        ),
    )(block_rows, block_cols, counts, block_tiles, start)


def solution(mesh):
    in_specs = (
        P("row", "col", None, None), P("row", "col"), P("row", "col"), P("row", "col"), P("col", None),
    )
    out_specs = (P(("row", "col"), None), P(("col", "row"), None))
    return jax.shard_map(shards, mesh=mesh, in_specs=in_specs, out_specs=out_specs, check_vma=False)
```

```python
import functools

import jax
import jax.numpy as jnp
from jax import lax
from jax.experimental import pallas as pl
from jax.experimental.pallas import tpu as pltpu
from jax.sharding import PartitionSpec as P

BLOCK = 128
BRD = 16
BCD = 8
NB = 20
HALF = 128
TOTAL = 32768.0
F32 = jnp.float32
BF16 = jnp.bfloat16


TO_OWNER = (5, -5, 2, -2, 1, -1)
RELAYED = (3, 2, -2, 1, -1)


def kernel(
    rows_ref, cols_ref, counts_ref, tiles_ref, start_ref, image_ref, basis_ref,
    srows, scols, scount, tab, ptab, tabv, ptabv, tl_own, tl_in, dense, bas, zsnd, zrcv, yt, acc,
    zc, r1, s2, r2, zfin, nbuf, ex_i, ex_b,
    pre_send, pre_recv, loc_sem, zs, zr, xs, xr, ns, nr, es, er,
):
    row = lax.axis_index("row")
    col = lax.axis_index("col")
    x, y = row // 4, row % 4
    z, c = col // 2, col % 2
    sg = 1 - 2 * c

    def at(xx, yy, zz, cc):
        return (((xx + 4) % 4) * 4 + (yy + 4) % 4, ((zz + 16) % 16) * 2 + cc)

    def zpos(e):
        return (z + sg * e + 16) % 16

    def zdev(e):
        return (row, zpos(e) * 2 + c)

    def remote(src, dst, ssem, rsem, dev):
        return pltpu.make_async_remote_copy(
            src_ref=src, dst_ref=dst, send_sem=ssem, recv_sem=rsem,
            device_id=dev, device_id_type=pl.DeviceIdType.MESH,
        )

    partner = (row, z * 2 + 1 - c)
    pending = []

    def norm_dev(stage, k):
        if stage == 0:
            return ((row + k) % 16, col)
        return (row, ((z + k) % 16) * 2 + c)

    barrier = pltpu.get_barrier_semaphore()

    def greet(dev):
        pl.semaphore_signal(barrier, inc=1, device_id=dev, device_id_type=pl.DeviceIdType.MESH)

    greet(partner)

    def greet_line(k, carry):
        greet(zdev(k))
        greet(zdev(-k))
        greet(at(x + k, y, z, c))
        greet(at(x, y + k, z, c))
        return carry

    lax.fori_loop(1, 4, greet_line, 0)

    local = [
        pltpu.make_async_copy(rows_ref, srows, loc_sem.at[0]),
        pltpu.make_async_copy(cols_ref, scols, loc_sem.at[1]),
        pltpu.make_async_copy(counts_ref, scount, loc_sem.at[2]),
        pltpu.make_async_copy(tiles_ref.at[0], tl_own.at[pl.ds(0, NB)], loc_sem.at[3]),
    ]
    for copy in local:
        copy.start()
    mine = pl.ds(pl.multiple_of(c * HALF, HALF), HALF)
    theirs = pl.ds(pl.multiple_of((1 - c) * HALF, HALF), HALF)
    own_start = pltpu.make_async_copy(start_ref.at[:, :, :, mine], bas.at[0, c], loc_sem.at[4])
    own_start.start()
    zero_tile = jnp.zeros((BLOCK, BLOCK), BF16)
    tl_own[NB] = zero_tile
    tl_in[NB] = zero_tile

    for copy in local[:3]:
        copy.wait()
    places = lax.broadcasted_iota(jnp.int32, (1, BRD * BCD), 1)
    slot_of = jnp.full((1, BRD * BCD), NB, jnp.int32)
    for slot in range(NB):
        place = jnp.where(slot < scount[0, 0], srows[0, slot] * BCD + scols[0, slot], -1)
        slot_of = jnp.where(places == place, slot, slot_of)
    tabv[...] = slot_of
    table_own = pltpu.make_async_copy(tabv, tab, loc_sem.at[5])
    table_own.start()

    pl.semaphore_wait(barrier, 13)
    pre = [
        remote(tabv, ptabv, pre_send.at[0], pre_recv.at[0], partner),
        remote(tiles_ref.at[0], tl_in.at[pl.ds(0, NB)], pre_send.at[1], pre_recv.at[1], partner),
        remote(start_ref.at[:, :, :, theirs], bas.at[0, c], pre_send.at[2], pre_recv.at[2], partner),
    ]
    for copy in pre:
        copy.start()

    def build(which, tl, table):
        def one_row(i, carry):
            for j in range(BCD):
                dense[which, i, :, j * BLOCK : (j + 1) * BLOCK] = tl[table[0, i * BCD + j]]
            return carry

        lax.fori_loop(0, BRD, one_row, 0)

    table_own.wait()
    local[3].wait()
    build(c, tl_own, tab)
    pre[0].wait_recv()
    table_in = pltpu.make_async_copy(ptabv, ptab, loc_sem.at[6])
    table_in.start()
    table_in.wait()
    pre[1].wait_recv()
    build(1 - c, tl_in, ptab)
    remote(start_ref.at[:, :, :, theirs], bas.at[0, 1 - c], pre_send.at[2], pre_recv.at[2], partner).wait_recv()
    own_start.wait()
    for copy in pre:
        copy.wait_send()

    def product(it, d):
        left = bas[it, 0].reshape(1024, HALF)
        right = bas[it, 1].reshape(1024, HALF)
        return jnp.dot(dense[0, d], left, preferred_element_type=F32) + jnp.dot(
            dense[1, d], right, preferred_element_type=F32
        )

    def rs_launch(it, m, group, owner, e):
        zsnd[it, m] = product(it, zpos(owner)).astype(BF16)
        rs_send(it, m, group, e)

    def rs_send(it, m, group, e):
        remote(zsnd.at[it, m], zrcv.at[it, m], zs.at[it, 0], zr.at[it, group], zdev(e)).start()

    def rs_arrived(it, group, begin, count):
        part = zrcv.at[it, pl.ds(begin, count)]
        remote(part, part, zs.at[it, 0], zr.at[it, group], zdev(1)).wait_recv()
        return jnp.sum(zrcv[it, begin : begin + count].astype(F32), axis=0)

    def z_reduce(it, late):
        rs_launch(it, 0, 0, 8, 3)

        def outer(k, carry):
            m = 2 * k
            rs_launch(it, m + 1, 0, 7 - k, 2 - k)
            rs_launch(it, m + 5, 1, k - 7, k - 2)
            rs_launch(it, m + 2, 0, 3 + k, k - 2)
            rs_launch(it, m + 6, 1, -3 - k, 2 - k)
            return carry

        lax.fori_loop(0, 2, outer, 0)

        def near(k, carry):
            m = 11 + 2 * k
            rs_launch(it, m, 2, 2 - k, 2 - k)
            rs_launch(it, m + 1, 2, k - 2, k - 2)
            return carry

        lax.fori_loop(0, 2, near, 0)
        ahead = product(it, zpos(5))
        behind = product(it, zpos(-5))
        own = product(it, z)
        late()
        zsnd[it, 9] = (ahead + rs_arrived(it, 0, 0, 5)).astype(BF16)
        rs_send(it, 9, 2, 5)
        zsnd[it, 10] = (behind + rs_arrived(it, 1, 5, 4)).astype(BF16)
        rs_send(it, 10, 2, -5)
        return own + rs_arrived(it, 2, 9, 6)

    def z_drain(it, phase):
        part = (zsnd if phase == 0 else yt).at[it, pl.ds(0, 15)]
        remote(part, part, zs.at[it, phase], zr.at[it, 0], zdev(1)).wait_send()

    def ag_send(it, group, owner, e):
        piece = yt.at[it, zpos(owner)]
        remote(piece, piece, zs.at[it, 1], zr.at[it, group], zdev(e)).start()

    def ag_arrived(it, group, count):
        part = yt.at[it, pl.ds(0, count)]
        remote(part, part, zs.at[it, 1], zr.at[it, group], zdev(1)).wait_recv()

    def add_products(it, pieces, first):
        for which in (0, 1):
            for part in range(2):
                cols = pl.ds(part * 512, 512)
                left = jnp.concatenate([yt[it, zpos(e)] for e in pieces], axis=1)
                right = jnp.concatenate([dense[which, zpos(e), :, cols] for e in pieces], axis=0)
                term = jnp.dot(left, right, preferred_element_type=F32)
                acc[which, :, cols] = term if first else acc[which, :, cols] + term

    def z_gather(it, late):
        for i, e in enumerate(TO_OWNER):
            ag_send(it, 3 + min(i, 2), 0, e)
        late()
        ag_arrived(it, 3, 1)
        for e in RELAYED:
            ag_send(it, 6 if abs(e) == 1 else 7, -5, e)
        ag_arrived(it, 4, 1)
        for e in RELAYED[1:]:
            ag_send(it, 6 if abs(e) == 1 else 7, 5, e)
        ag_arrived(it, 5, 4)
        add_products(it, [-5, 5, -2, 2, -1, 1, 0], True)
        ag_arrived(it, 6, 4)
        add_products(it, [-6, -4, 4, 6], False)
        ag_arrived(it, 7, 5)
        add_products(it, [-7, -3, 3, 7, -8], False)

    def coord(axis):
        return x if axis == 0 else y

    def axis_dev(axis, k):
        if axis == 0:
            return at(x + k, y, z, c)
        return at(x, y + k, z, c)

    def xy_copy(it, phase, stage, h, k, axis, src, dst):
        p = it * (2 - phase)
        return remote(src, dst, xs.at[p, stage], xr.at[p, stage, h], axis_dev(axis, k))

    def xy_drain(it, phase, stage, part):
        xy_copy(it, phase, stage, 0, 1, 0, part, part).wait_send()

    def xy_reduce(it, stage, axes, buf, landing):
        for k in (2, 1, 3):
            for h in (0, 1):
                group = (coord(axes[h]) + k) % 4
                xy_copy(it, 0, stage, h, k, axes[h], buf.at[it, h, group], landing.at[it, h, k - 1]).start()
        totals = []
        for h in (0, 1):
            part = landing.at[it, h]
            xy_copy(it, 0, stage, h, 1, 0, part, part).wait_recv()
            total = buf[it, h, coord(axes[h])].astype(F32)
            for k in range(3):
                total = total + landing[it, h, k].astype(F32)
            totals.append(total)
        pending.append(functools.partial(xy_drain, it, 0, stage, buf.at[it, :, pl.ds(0, 3)]))
        return totals

    def piece_ref(it, h, stage, axis, g):
        if stage == 0:
            return bas.at[it, h, g, y] if axis == 0 else bas.at[it, h, x, g]
        return bas.at[it, h, g] if axis == 0 else bas.at[it, h, :, g]

    def three(it, stage, h):
        return bas.at[it, h, 0, pl.ds(0, 3)] if stage == 0 else bas.at[it, h, pl.ds(0, 3)]

    def xy_gather(it, stage, axes, late):
        for k in (2, 1, 3):
            for h in (0, 1):
                ref = piece_ref(it, h, stage, axes[h], coord(axes[h]))
                xy_copy(it, 1, stage, h, k, axes[h], ref, ref).start()
        pending.append(functools.partial(xy_drain, it, 1, stage, three(it, stage, slice(None))))
        late()
        for h in (0, 1):
            part = three(it, stage, h)
            xy_copy(it, 1, stage, h, 1, 0, part, part).wait_recv()

    def norm_copy(it, stage, src, dst, k):
        return remote(src, dst, ns.at[it, stage], nr.at[it, stage], norm_dev(stage, k))

    def norm_start(it, stage, value):
        nbuf[it, stage, 0] = jnp.broadcast_to(value, (8, HALF))

        def one(k, carry):
            norm_copy(it, stage, nbuf.at[it, stage, 0], nbuf.at[it, stage, k], k).start()
            return carry

        lax.fori_loop(1, 16, one, 0)
        rest = nbuf.at[it, stage, pl.ds(1, 15)]
        pending.append(norm_copy(it, stage, rest, rest, 1).wait_send)

    def norm_finish(it, stage):
        rest = nbuf.at[it, stage, pl.ds(1, 15)]
        norm_copy(it, stage, rest, rest, 1).wait_recv()
        return jnp.sum(nbuf[it, stage], axis=0)[0:1]

    def scale_of(total):
        return lax.rsqrt(total / TOTAL + 1e-06)

    lane = lax.broadcasted_iota(jnp.int32, (HALF, BLOCK), 1) < 64

    for it in (0, 1):
        def share_norm():
            if it == 1:
                norm_start(0, 1, norm_finish(0, 0))

        own = z_reduce(it, share_norm)
        pending.append(functools.partial(z_drain, it, 0))
        if it == 1:
            own = own * scale_of(norm_finish(0, 1))
        own = own.astype(BF16)

        yt[it, z] = own.astype(F32).T.astype(BF16)

        def share_image():
            if it == 1:
                ex_i[0] = own[:64]
                ex_i[1] = own[64:]
                remote(ex_i.at[1 - c], ex_i.at[2], es.at[0], er.at[0], partner).start()

        z_gather(it, share_image)
        pending.append(functools.partial(z_drain, it, 1))
        for j in range(BCD):
            blk = slice(j * BLOCK, (j + 1) * BLOCK)
            zero_half = acc[0, :, blk]
            one_half = acc[1, :, blk]
            pair = (
                jnp.where(lane, zero_half, pltpu.roll(one_half, 64, 1)).astype(BF16),
                jnp.where(lane, pltpu.roll(zero_half, 64, 1), one_half).astype(BF16),
            )
            for odd in (0, 1):
                xx, yy = divmod(2 * j + odd, 4)
                zc[it, 0, xx, yy] = pair[odd][:64]
                zc[it, 1, yy, xx] = pair[odd][64:]
        first = xy_reduce(it, 0, (0, 1), zc, r1)
        for h in (0, 1):
            s2[it, h] = first[h].astype(BF16)
        second = xy_reduce(it, 1, (1, 0), s2, r2)
        rows = jnp.concatenate(second, axis=0).T
        squares = jnp.sum(rows * rows, axis=0, keepdims=True)
        if it == 0:
            low = rows.astype(BF16)
            bas[1, 0, x, y] = low[:64]
            bas[1, 1, x, y] = low[64:]
            xy_gather(1, 0, (1, 0), functools.partial(norm_start, 0, 0, squares))
            xy_gather(1, 1, (0, 1), lambda: None)
        else:
            norm_start(1, 0, squares)
            zfin[...] = rows
            remote(ex_i.at[1 - c], ex_i.at[2], es.at[0], er.at[0], partner).wait()
            image_ref[:, mine] = ex_i[c]
            image_ref[:, theirs] = ex_i[2]
            norm_start(1, 1, norm_finish(1, 0))
            low = (zfin[...] * scale_of(norm_finish(1, 1))).astype(BF16)
            ex_b[0] = low[:64]
            ex_b[1] = low[64:]
            swap = remote(ex_b.at[1 - c], ex_b.at[2], es.at[1], er.at[1], partner)
            swap.start()
            basis_ref[:, mine] = ex_b[c]
            swap.wait()
            basis_ref[:, theirs] = ex_b[2]

    for drain in pending:
        drain()


def shards(block_tiles, block_rows, block_cols, counts, start_basis):
    start = start_basis.reshape(4, 4, 64, 2 * HALF)
    dma = pltpu.SemaphoreType.DMA
    vmem = pltpu.VMEM
    smem = pltpu.SMEM
    scratch = [
        smem((1, NB), jnp.int32), smem((1, NB), jnp.int32), smem((1, 1), jnp.int32),
        smem((1, 128), jnp.int32), smem((1, 128), jnp.int32),
        vmem((1, 128), jnp.int32), vmem((1, 128), jnp.int32),
        vmem((NB + 1, BLOCK, BLOCK), BF16),
        vmem((NB + 1, BLOCK, BLOCK), BF16),
        vmem((2, BRD, BLOCK, 1024), BF16),
        vmem((2, 2, 4, 4, 64, HALF), BF16),
        vmem((2, 15, BLOCK, HALF), BF16),
        vmem((2, 15, BLOCK, HALF), BF16),
        vmem((2, 16, HALF, BLOCK), BF16),
        vmem((2, HALF, 1024), F32),
        vmem((2, 2, 4, 4, 64, BLOCK), BF16),
        vmem((2, 2, 3, 4, 64, BLOCK), BF16),
        vmem((2, 2, 4, 64, BLOCK), BF16),
        vmem((2, 2, 3, 64, BLOCK), BF16),
        vmem((BLOCK, HALF), F32),
        vmem((2, 2, 16, 8, HALF), F32),
        vmem((3, 64, HALF), BF16),
        vmem((3, 64, HALF), BF16),
        dma((3,)), dma((3,)), dma((7,)),
        dma((2, 2)), dma((2, 8)),
        dma((3, 2)), dma((3, 2, 2)),
        dma((2, 2)), dma((2, 2)),
        dma((2,)), dma((2,)),
    ]
    anywhere = pl.BlockSpec(memory_space=pl.ANY)
    in_vmem = pl.BlockSpec(memory_space=pltpu.VMEM)
    return pl.pallas_call(
        kernel,
        out_shape=(
            jax.ShapeDtypeStruct((64, 2 * HALF), BF16),
            jax.ShapeDtypeStruct((64, 2 * HALF), BF16),
        ),
        in_specs=[anywhere] * 5,
        out_specs=(in_vmem, in_vmem),
        scratch_shapes=scratch,
        compiler_params=pltpu.CompilerParams(
            collective_id=0, has_side_effects=True, vmem_limit_bytes=63 * 1024 * 1024
        ),
    )(block_rows, block_cols, counts, block_tiles, start)


def solution(mesh):
    in_specs = (
        P("row", "col", None, None), P("row", "col"), P("row", "col"), P("row", "col"), P("col", None),
    )
    out_specs = (P(("row", "col"), None), P(("col", "row"), None))
    return jax.shard_map(shards, mesh=mesh, in_specs=in_specs, out_specs=out_specs, check_vma=False)
```

```python
import functools

import jax
import jax.numpy as jnp
from jax import lax
from jax.experimental import pallas as pl
from jax.experimental.pallas import tpu as pltpu
from jax.sharding import PartitionSpec as P

BLOCK = 128
BRD = 16
BCD = 8
NB = 20
HALF = 128
TOTAL = 32768.0
F32 = jnp.float32
BF16 = jnp.bfloat16


TO_OWNER = (5, -5, 3, -3, 2, -2, 1, -1)
RELAYED = (3, 2, 1, -1)


def kernel(
    rows_ref, cols_ref, counts_ref, tiles_ref, start_ref, image_ref, basis_ref,
    srows, scols, scount, tab, ptab, tabv, ptabv, tl_own, tl_in, dense, bas, zsnd, zrcv, yt, acc,
    zc, r1, s2, r2, zfin, nbuf, ex_i, ex_b,
    pre_send, pre_recv, loc_sem, zs, zr, xs, xr, ns, nr, es, er, turn,
):
    row = lax.axis_index("row")
    col = lax.axis_index("col")
    x, y = row // 4, row % 4
    z, c = col // 2, col % 2
    sg = 1 - 2 * c

    def at(xx, yy, zz, cc):
        return (((xx + 4) % 4) * 4 + (yy + 4) % 4, ((zz + 16) % 16) * 2 + cc)

    def zpos(e):
        return (z + sg * e + 16) % 16

    def zdev(e):
        return (row, zpos(e) * 2 + c)

    def remote(src, dst, ssem, rsem, dev):
        return pltpu.make_async_remote_copy(
            src_ref=src, dst_ref=dst, send_sem=ssem, recv_sem=rsem,
            device_id=dev, device_id_type=pl.DeviceIdType.MESH,
        )

    partner = (row, z * 2 + 1 - c)
    pending = []

    def norm_dev(stage, k):
        if stage == 0:
            return ((row + k) % 16, col)
        return (row, ((z + k) % 16) * 2 + c)

    barrier = pltpu.get_barrier_semaphore()

    def greet(dev):
        pl.semaphore_signal(barrier, inc=1, device_id=dev, device_id_type=pl.DeviceIdType.MESH)

    greet(partner)

    def greet_line(k, carry):
        greet(zdev(k))
        greet(zdev(-k))
        greet(at(x + k, y, z, c))
        greet(at(x, y + k, z, c))
        return carry

    lax.fori_loop(1, 4, greet_line, 0)

    local = [
        pltpu.make_async_copy(rows_ref, srows, loc_sem.at[0]),
        pltpu.make_async_copy(cols_ref, scols, loc_sem.at[1]),
        pltpu.make_async_copy(counts_ref, scount, loc_sem.at[2]),
        pltpu.make_async_copy(tiles_ref.at[0], tl_own.at[pl.ds(0, NB)], loc_sem.at[3]),
    ]
    for copy in local:
        copy.start()
    mine = pl.ds(pl.multiple_of(c * HALF, HALF), HALF)
    theirs = pl.ds(pl.multiple_of((1 - c) * HALF, HALF), HALF)
    own_start = pltpu.make_async_copy(start_ref.at[:, :, :, mine], bas.at[0, c], loc_sem.at[4])
    own_start.start()
    zero_tile = jnp.zeros((BLOCK, BLOCK), BF16)
    tl_own[NB] = zero_tile
    tl_in[NB] = zero_tile

    for copy in local[:3]:
        copy.wait()
    places = lax.broadcasted_iota(jnp.int32, (1, BRD * BCD), 1)
    slot_of = jnp.full((1, BRD * BCD), NB, jnp.int32)
    for slot in range(NB):
        place = jnp.where(slot < scount[0, 0], srows[0, slot] * BCD + scols[0, slot], -1)
        slot_of = jnp.where(places == place, slot, slot_of)
    tabv[...] = slot_of
    table_own = pltpu.make_async_copy(tabv, tab, loc_sem.at[5])
    table_own.start()

    pl.semaphore_wait(barrier, 13)
    pre = [
        remote(tabv, ptabv, pre_send.at[0], pre_recv.at[0], partner),
        remote(tiles_ref.at[0], tl_in.at[pl.ds(0, NB)], pre_send.at[1], pre_recv.at[1], partner),
        remote(start_ref.at[:, :, :, theirs], bas.at[0, c], pre_send.at[2], pre_recv.at[2], partner),
    ]
    for copy in pre:
        copy.start()

    def build(which, tl, table):
        def one_row(i, carry):
            for j in range(BCD):
                dense[which, i, :, j * BLOCK : (j + 1) * BLOCK] = tl[table[0, i * BCD + j]]
            return carry

        lax.fori_loop(0, BRD, one_row, 0)

    table_own.wait()
    local[3].wait()
    build(c, tl_own, tab)
    pre[0].wait_recv()
    table_in = pltpu.make_async_copy(ptabv, ptab, loc_sem.at[6])
    table_in.start()
    table_in.wait()
    pre[1].wait_recv()
    build(1 - c, tl_in, ptab)
    remote(start_ref.at[:, :, :, theirs], bas.at[0, 1 - c], pre_send.at[2], pre_recv.at[2], partner).wait_recv()
    own_start.wait()
    for copy in pre:
        copy.wait_send()

    def product(it, d):
        left = bas[it, 0].reshape(1024, HALF)
        right = bas[it, 1].reshape(1024, HALF)
        return jnp.dot(dense[0, d], left, preferred_element_type=F32) + jnp.dot(
            dense[1, d], right, preferred_element_type=F32
        )

    def rs_launch(it, m, group, owner, e):
        zsnd[it, m] = product(it, zpos(owner)).astype(BF16)
        rs_send(it, m, group, e)

    def rs_send(it, m, group, e):
        remote(zsnd.at[it, m], zrcv.at[it, m], zs.at[it, 0], zr.at[it, group], zdev(e)).start()

    def rs_arrived(it, group, begin, count):
        part = zrcv.at[it, pl.ds(begin, count)]
        remote(part, part, zs.at[it, 0], zr.at[it, group], zdev(1)).wait_recv()
        return jnp.sum(zrcv[it, begin : begin + count].astype(F32), axis=0)

    def z_reduce(it, late):
        rs_launch(it, 0, 0, 8, 3)

        def outer(k, carry):
            m = 2 * k
            rs_launch(it, m + 1, 0, 7 - k, 2 - k)
            rs_launch(it, m + 5, 1, k - 7, k - 2)
            rs_launch(it, m + 2, 0, 3 + k, k - 2)
            rs_launch(it, m + 6, 1, -3 - k, 2 - k)
            return carry

        lax.fori_loop(0, 2, outer, 0)

        def near(k, carry):
            m = 11 + 2 * k
            rs_launch(it, m, 2, 2 - k, 2 - k)
            rs_launch(it, m + 1, 2, k - 2, k - 2)
            return carry

        lax.fori_loop(0, 2, near, 0)
        ahead = product(it, zpos(5))
        behind = product(it, zpos(-5))
        own = product(it, z)
        late()
        zsnd[it, 9] = (ahead + rs_arrived(it, 0, 0, 5)).astype(BF16)
        rs_send(it, 9, 2, 5)
        zsnd[it, 10] = (behind + rs_arrived(it, 1, 5, 4)).astype(BF16)
        rs_send(it, 10, 2, -5)
        return own + rs_arrived(it, 2, 9, 6)

    def z_drain(it, phase):
        part = (zsnd if phase == 0 else yt).at[it, pl.ds(0, 15)]
        remote(part, part, zs.at[it, phase], zr.at[it, 0], zdev(1)).wait_send()

    def ag_send(it, group, owner, e):
        piece = yt.at[it, zpos(owner)]
        remote(piece, piece, zs.at[it, 1], zr.at[it, group], zdev(e)).start()

    def ag_arrived(it, group, count):
        part = yt.at[it, pl.ds(0, count)]
        remote(part, part, zs.at[it, 1], zr.at[it, group], zdev(1)).wait_recv()

    def add_products(it, pieces, first):
        for which in (0, 1):
            for part in range(2):
                cols = pl.ds(part * 512, 512)
                left = jnp.concatenate([yt[it, zpos(e)] for e in pieces], axis=1)
                right = jnp.concatenate([dense[which, zpos(e), :, cols] for e in pieces], axis=0)
                term = jnp.dot(left, right, preferred_element_type=F32)
                acc[which, :, cols] = term if first else acc[which, :, cols] + term

    def z_gather(it, late):
        for i, e in enumerate(TO_OWNER):
            ag_send(it, 3 + min(i, 2), 0, e)
        late()
        ag_arrived(it, 3, 1)
        for e in RELAYED:
            ag_send(it, 6 if abs(e) == 1 else 7, -5, e)
        ag_arrived(it, 4, 1)
        for e in RELAYED[1:]:
            ag_send(it, 6 if abs(e) == 1 else 7, 5, -e)
        ag_arrived(it, 5, 6)
        add_products(it, [-5, 5, -3, 3, -2, 2, -1, 1, 0], True)
        ag_arrived(it, 6, 4)
        add_products(it, [-6, -4, 4, 6], False)
        ag_arrived(it, 7, 3)
        add_products(it, [-7, 7, -8], False)

    def coord(axis):
        return x if axis == 0 else y

    def axis_dev(axis, k):
        if axis == 0:
            return at(x + k, y, z, c)
        return at(x, y + k, z, c)

    def xy_copy(it, phase, stage, h, k, axis, src, dst):
        p = it * (2 - phase)
        return remote(src, dst, xs.at[p, stage], xr.at[p, stage, h], axis_dev(axis, k))

    def xy_drain(it, phase, stage, part):
        xy_copy(it, phase, stage, 0, 1, 0, part, part).wait_send()

    def xy_reduce(it):
        def send(stage, h, buf, landing):
            axis = (h + stage) % 2
            for k in (2, 1, 3):
                group = (coord(axis) + k) % 4
                xy_copy(it, 0, stage, h, k, axis, buf.at[it, h, group], landing.at[it, h, k - 1]).start()

        def total(stage, h, buf, landing):
            part = landing.at[it, h]
            xy_copy(it, 0, stage, h, 1, 0, part, part).wait_recv()
            value = buf[it, h, coord((h + stage) % 2)].astype(F32)
            for k in range(3):
                value = value + landing[it, h, k].astype(F32)
            return value

        for h in range(4):
            send(0, h, zc, r1)
        for h in range(4):
            s2[it, h] = total(0, h, zc, r1).astype(BF16)
            send(1, h, s2, r2)
        pending.append(functools.partial(xy_drain, it, 0, 0, zc.at[it, :, pl.ds(0, 3)]))
        pending.append(functools.partial(xy_drain, it, 0, 1, s2.at[it, :, pl.ds(0, 3)]))
        return [total(1, h, s2, r2) for h in range(4)]

    def piece_ref(it, h, stage, axis, g):
        if stage == 0:
            return bas.at[it, h, g, y] if axis == 0 else bas.at[it, h, x, g]
        return bas.at[it, h, g] if axis == 0 else bas.at[it, h, :, g]

    def three(it, stage, h):
        return bas.at[it, h, 0, pl.ds(0, 3)] if stage == 0 else bas.at[it, h, pl.ds(0, 3)]

    def xy_gather(it, stage, axes, late):
        for k in (2, 1, 3):
            for h in (0, 1):
                ref = piece_ref(it, h, stage, axes[h], coord(axes[h]))
                xy_copy(it, 1, stage, h, k, axes[h], ref, ref).start()
        pending.append(functools.partial(xy_drain, it, 1, stage, three(it, stage, slice(None))))
        late()
        for h in (0, 1):
            part = three(it, stage, h)
            xy_copy(it, 1, stage, h, 1, 0, part, part).wait_recv()

    def norm_copy(it, stage, src, dst, k):
        return remote(src, dst, ns.at[it, stage], nr.at[it, stage], norm_dev(stage, k))

    def norm_start(it, stage, value):
        nbuf[it, stage, 0] = jnp.broadcast_to(value, (8, HALF))

        def one(k, carry):
            norm_copy(it, stage, nbuf.at[it, stage, 0], nbuf.at[it, stage, k], k).start()
            return carry

        lax.fori_loop(1, 16, one, 0)
        rest = nbuf.at[it, stage, pl.ds(1, 15)]
        pending.append(norm_copy(it, stage, rest, rest, 1).wait_send)

    def norm_finish(it, stage):
        rest = nbuf.at[it, stage, pl.ds(1, 15)]
        norm_copy(it, stage, rest, rest, 1).wait_recv()
        return jnp.sum(nbuf[it, stage], axis=0)[0:1]

    def scale_of(total):
        return lax.rsqrt(total / TOTAL + 1e-06)

    def give_turn():
        @pl.when(c == 0)
        def _():
            pl.semaphore_signal(turn, inc=1, device_id=partner, device_id_type=pl.DeviceIdType.MESH)

    @pl.when(c == 1)
    def _():
        pl.semaphore_wait(turn, 1)

    lane = lax.broadcasted_iota(jnp.int32, (HALF, BLOCK), 1) < 64

    for it in (0, 1):
        def share_norm():
            if it == 1:
                norm_start(0, 1, norm_finish(0, 0))

        own = z_reduce(it, share_norm)
        if it == 0:
            give_turn()
        pending.append(functools.partial(z_drain, it, 0))
        if it == 1:
            own = own * scale_of(norm_finish(0, 1))
        own = own.astype(BF16)

        yt[it, z] = own.astype(F32).T.astype(BF16)

        def share_image():
            if it == 1:
                ex_i[0] = own[:64]
                ex_i[1] = own[64:]
                remote(ex_i.at[1 - c], ex_i.at[2], es.at[0], er.at[0], partner).start()

        z_gather(it, share_image)
        pending.append(functools.partial(z_drain, it, 1))
        for j in range(BCD):
            blk = slice(j * BLOCK, (j + 1) * BLOCK)
            zero_half = acc[0, :, blk]
            one_half = acc[1, :, blk]
            pair = (
                jnp.where(lane, zero_half, pltpu.roll(one_half, 64, 1)).astype(BF16),
                jnp.where(lane, pltpu.roll(zero_half, 64, 1), one_half).astype(BF16),
            )
            for odd in (0, 1):
                xx, yy = divmod(2 * j + odd, 4)
                for h in range(4):
                    xy = (yy, xx) if h % 2 else (xx, yy)
                    zc[it, h, xy[0], xy[1]] = pair[odd][32 * h : 32 * h + 32]
        second = xy_reduce(it)
        rows = jnp.concatenate(second, axis=0).T
        squares = jnp.sum(rows * rows, axis=0, keepdims=True)
        if it == 0:
            low = rows.astype(BF16)
            bas[1, 0, x, y] = low[:64]
            bas[1, 1, x, y] = low[64:]
            xy_gather(1, 0, (1, 0), functools.partial(norm_start, 0, 0, squares))
            xy_gather(1, 1, (0, 1), lambda: None)
        else:
            norm_start(1, 0, squares)
            zfin[...] = rows
            remote(ex_i.at[1 - c], ex_i.at[2], es.at[0], er.at[0], partner).wait()
            image_ref[:, mine] = ex_i[c]
            image_ref[:, theirs] = ex_i[2]
            norm_start(1, 1, norm_finish(1, 0))
            low = (zfin[...] * scale_of(norm_finish(1, 1))).astype(BF16)
            ex_b[0] = low[:64]
            ex_b[1] = low[64:]
            swap = remote(ex_b.at[1 - c], ex_b.at[2], es.at[1], er.at[1], partner)
            swap.start()
            basis_ref[:, mine] = ex_b[c]
            swap.wait()
            basis_ref[:, theirs] = ex_b[2]

    for drain in pending:
        drain()


def shards(block_tiles, block_rows, block_cols, counts, start_basis):
    start = start_basis.reshape(4, 4, 64, 2 * HALF)
    dma = pltpu.SemaphoreType.DMA
    vmem = pltpu.VMEM
    smem = pltpu.SMEM
    scratch = [
        smem((1, NB), jnp.int32), smem((1, NB), jnp.int32), smem((1, 1), jnp.int32),
        smem((1, 128), jnp.int32), smem((1, 128), jnp.int32),
        vmem((1, 128), jnp.int32), vmem((1, 128), jnp.int32),
        vmem((NB + 1, BLOCK, BLOCK), BF16),
        vmem((NB + 1, BLOCK, BLOCK), BF16),
        vmem((2, BRD, BLOCK, 1024), BF16),
        vmem((2, 2, 4, 4, 64, HALF), BF16),
        vmem((2, 15, BLOCK, HALF), BF16),
        vmem((2, 15, BLOCK, HALF), BF16),
        vmem((2, 16, HALF, BLOCK), BF16),
        vmem((2, HALF, 1024), F32),
        vmem((2, 4, 4, 4, 32, BLOCK), BF16),
        vmem((2, 4, 3, 4, 32, BLOCK), BF16),
        vmem((2, 4, 4, 32, BLOCK), BF16),
        vmem((2, 4, 3, 32, BLOCK), BF16),
        vmem((BLOCK, HALF), F32),
        vmem((2, 2, 16, 8, HALF), F32),
        vmem((3, 64, HALF), BF16),
        vmem((3, 64, HALF), BF16),
        dma((3,)), dma((3,)), dma((7,)),
        dma((2, 2)), dma((2, 8)),
        dma((3, 2)), dma((3, 2, 4)),
        dma((2, 2)), dma((2, 2)),
        dma((2,)), dma((2,)),
        pltpu.SemaphoreType.REGULAR,
    ]
    anywhere = pl.BlockSpec(memory_space=pl.ANY)
    in_vmem = pl.BlockSpec(memory_space=pltpu.VMEM)
    return pl.pallas_call(
        kernel,
        out_shape=(
            jax.ShapeDtypeStruct((64, 2 * HALF), BF16),
            jax.ShapeDtypeStruct((64, 2 * HALF), BF16),
        ),
        in_specs=[anywhere] * 5,
        out_specs=(in_vmem, in_vmem),
        scratch_shapes=scratch,
        compiler_params=pltpu.CompilerParams(
            collective_id=0, has_side_effects=True, vmem_limit_bytes=538 * 1024 * 1024 // 10
        ),
    )(block_rows, block_cols, counts, block_tiles, start)


def solution(mesh):
    in_specs = (
        P("row", "col", None, None), P("row", "col"), P("row", "col"), P("row", "col"), P("col", None),
    )
    out_specs = (P(("row", "col"), None), P(("col", "row"), None))
    return jax.shard_map(shards, mesh=mesh, in_specs=in_specs, out_specs=out_specs, check_vma=False)
```

```python
import functools

import jax
import jax.numpy as jnp
from jax import lax
from jax.experimental import pallas as pl
from jax.experimental.pallas import tpu as pltpu
from jax.sharding import PartitionSpec as P

BLOCK = 128
BRD = 16
BCD = 8
NB = 20
HALF = 128
TOTAL = 32768.0
F32 = jnp.float32
BF16 = jnp.bfloat16


TO_OWNER = (5, -5, 3, -3, 2, -2, 1, -1)
RELAYED = (3, 2, 1, -1)

FAR_FIRST = (
    (10, 9, 11, 6, 14, 5, 7, 13, 15, 8, 2, 1, 3, 4, 12),
    (8, 9, 7, 10, 6, 11, 5, 12, 4, 13, 3, 14, 2, 15, 1),
)


def kernel(
    rows_ref, cols_ref, counts_ref, tiles_ref, start_ref, image_ref, basis_ref,
    srows, scols, scount, tab, ptab, tabv, ptabv, tl_own, tl_in, dense, bas, zsnd, zrcv, yt, acc,
    zc, r1, s2, r2, zfin, nbuf, ex_i, ex_b,
    pre_send, pre_recv, loc_sem, zs, zr, xs, xr, ns, nr, es, er, turn,
):
    row = lax.axis_index("row")
    col = lax.axis_index("col")
    x, y = row // 4, row % 4
    z, c = col // 2, col % 2
    sg = 1 - 2 * c

    def at(xx, yy, zz, cc):
        return (((xx + 4) % 4) * 4 + (yy + 4) % 4, ((zz + 16) % 16) * 2 + cc)

    def zpos(e):
        return (z + sg * e + 16) % 16

    def zdev(e):
        return (row, zpos(e) * 2 + c)

    def remote(src, dst, ssem, rsem, dev):
        return pltpu.make_async_remote_copy(
            src_ref=src, dst_ref=dst, send_sem=ssem, recv_sem=rsem,
            device_id=dev, device_id_type=pl.DeviceIdType.MESH,
        )

    partner = (row, z * 2 + 1 - c)
    pending = []

    def norm_dev(stage, k):
        if stage == 0:
            return at(x + k // 4, y + k % 4, z, c)
        return (row, ((z + k) % 16) * 2 + c)

    barrier = pltpu.get_barrier_semaphore()

    def greet(dev):
        pl.semaphore_signal(barrier, inc=1, device_id=dev, device_id_type=pl.DeviceIdType.MESH)

    greet(partner)

    def greet_line(k, carry):
        greet(zdev(k))
        greet(zdev(-k))
        greet(at(x + k, y, z, c))
        greet(at(x, y + k, z, c))
        return carry

    lax.fori_loop(1, 4, greet_line, 0)

    local = [
        pltpu.make_async_copy(rows_ref, srows, loc_sem.at[0]),
        pltpu.make_async_copy(cols_ref, scols, loc_sem.at[1]),
        pltpu.make_async_copy(counts_ref, scount, loc_sem.at[2]),
        pltpu.make_async_copy(tiles_ref.at[0], tl_own.at[pl.ds(0, NB)], loc_sem.at[3]),
    ]
    for copy in local:
        copy.start()
    mine = pl.ds(pl.multiple_of(c * HALF, HALF), HALF)
    theirs = pl.ds(pl.multiple_of((1 - c) * HALF, HALF), HALF)
    own_start = pltpu.make_async_copy(start_ref.at[:, :, :, mine], bas.at[0, c], loc_sem.at[4])
    own_start.start()
    zero_tile = jnp.zeros((BLOCK, BLOCK), BF16)
    tl_own[NB] = zero_tile
    tl_in[NB] = zero_tile

    for copy in local[:3]:
        copy.wait()
    places = lax.broadcasted_iota(jnp.int32, (1, BRD * BCD), 1)
    slot_of = jnp.full((1, BRD * BCD), NB, jnp.int32)
    for slot in range(NB):
        place = jnp.where(slot < scount[0, 0], srows[0, slot] * BCD + scols[0, slot], -1)
        slot_of = jnp.where(places == place, slot, slot_of)
    tabv[...] = slot_of
    table_own = pltpu.make_async_copy(tabv, tab, loc_sem.at[5])
    table_own.start()

    pl.semaphore_wait(barrier, 13)
    pre = [
        remote(tabv, ptabv, pre_send.at[0], pre_recv.at[0], partner),
        remote(tiles_ref.at[0], tl_in.at[pl.ds(0, NB)], pre_send.at[1], pre_recv.at[1], partner),
        remote(start_ref.at[:, :, :, theirs], bas.at[0, c], pre_send.at[2], pre_recv.at[2], partner),
    ]
    for copy in pre:
        copy.start()

    def build(which, tl, table):
        def one_row(i, carry):
            for j in range(BCD):
                dense[which, i, :, j * BLOCK : (j + 1) * BLOCK] = tl[table[0, i * BCD + j]]
            return carry

        lax.fori_loop(0, BRD, one_row, 0)

    table_own.wait()
    local[3].wait()
    build(c, tl_own, tab)
    pre[0].wait_recv()
    table_in = pltpu.make_async_copy(ptabv, ptab, loc_sem.at[6])
    table_in.start()
    table_in.wait()
    pre[1].wait_recv()
    build(1 - c, tl_in, ptab)
    remote(start_ref.at[:, :, :, theirs], bas.at[0, 1 - c], pre_send.at[2], pre_recv.at[2], partner).wait_recv()
    own_start.wait()
    for copy in pre:
        copy.wait_send()

    def product(it, d):
        left = bas[it, 0].reshape(1024, HALF)
        right = bas[it, 1].reshape(1024, HALF)
        return jnp.dot(dense[0, d], left, preferred_element_type=F32) + jnp.dot(
            dense[1, d], right, preferred_element_type=F32
        )

    def rs_launch(it, m, group, owner, e):
        zsnd[it, m] = product(it, zpos(owner)).astype(BF16)
        rs_send(it, m, group, e)

    def rs_send(it, m, group, e):
        remote(zsnd.at[it, m], zrcv.at[it, m], zs.at[it, 0], zr.at[it, group], zdev(e)).start()

    def rs_arrived(it, group, begin, count):
        part = zrcv.at[it, pl.ds(begin, count)]
        remote(part, part, zs.at[it, 0], zr.at[it, group], zdev(1)).wait_recv()
        return jnp.sum(zrcv[it, begin : begin + count].astype(F32), axis=0)

    def z_reduce(it, late):
        rs_launch(it, 0, 0, 8, 3)

        def outer(k, carry):
            m = 2 * k
            rs_launch(it, m + 1, 0, 7 - k, 2 - k)
            rs_launch(it, m + 5, 1, k - 7, k - 2)
            rs_launch(it, m + 2, 0, 3 + k, k - 2)
            rs_launch(it, m + 6, 1, -3 - k, 2 - k)
            return carry

        lax.fori_loop(0, 2, outer, 0)
        if it == 0:
            give_turn()

        def near(k, carry):
            m = 11 + 2 * k
            rs_launch(it, m, 2, 2 - k, 2 - k)
            rs_launch(it, m + 1, 2, k - 2, k - 2)
            return carry

        lax.fori_loop(0, 2, near, 0)
        ahead = product(it, zpos(5))
        behind = product(it, zpos(-5))
        own = product(it, z)
        late()
        zsnd[it, 9] = (ahead + rs_arrived(it, 0, 0, 5)).astype(BF16)
        rs_send(it, 9, 2, 5)
        zsnd[it, 10] = (behind + rs_arrived(it, 1, 5, 4)).astype(BF16)
        rs_send(it, 10, 2, -5)
        return own + rs_arrived(it, 2, 9, 6)

    def z_drain(it, phase):
        part = (zsnd if phase == 0 else yt).at[it, pl.ds(0, 15)]
        remote(part, part, zs.at[it, phase], zr.at[it, 0], zdev(1)).wait_send()

    def ag_send(it, group, owner, e):
        piece = yt.at[it, zpos(owner)]
        remote(piece, piece, zs.at[it, 1], zr.at[it, group], zdev(e)).start()

    def ag_arrived(it, group, count):
        part = yt.at[it, pl.ds(0, count)]
        remote(part, part, zs.at[it, 1], zr.at[it, group], zdev(1)).wait_recv()

    def add_products(it, pieces, first):
        for which in (0, 1):
            for part in range(2):
                cols = pl.ds(part * 512, 512)
                left = jnp.concatenate([yt[it, zpos(e)] for e in pieces], axis=1)
                right = jnp.concatenate([dense[which, zpos(e), :, cols] for e in pieces], axis=0)
                term = jnp.dot(left, right, preferred_element_type=F32)
                acc[which, :, cols] = term if first else acc[which, :, cols] + term

    def z_gather(it, late):
        for i, e in enumerate(TO_OWNER):
            ag_send(it, 3 + min(i, 2), 0, e)
        late()
        ag_arrived(it, 3, 1)
        for e in RELAYED:
            ag_send(it, 6 if abs(e) == 1 else 7, -5, e)
        ag_arrived(it, 4, 1)
        for e in RELAYED[1:]:
            ag_send(it, 6 if abs(e) == 1 else 7, 5, -e)
        ag_arrived(it, 5, 6)
        add_products(it, [-5, 5, -3, 3, -2, 2, -1, 1, 0], True)
        ag_arrived(it, 6, 4)
        add_products(it, [-6, -4, 4, 6], False)
        ag_arrived(it, 7, 3)
        add_products(it, [-7, 7, -8], False)

    def coord(axis):
        return x if axis == 0 else y

    def axis_dev(axis, k):
        if axis == 0:
            return at(x + k, y, z, c)
        return at(x, y + k, z, c)

    def xy_copy(it, phase, stage, h, k, axis, src, dst):
        p = it * (2 - phase)
        return remote(src, dst, xs.at[p, stage], xr.at[p, stage, h], axis_dev(axis, k))

    def xy_drain(it, phase, stage, part):
        xy_copy(it, phase, stage, 0, 1, 0, part, part).wait_send()

    def xy_reduce(it):
        def send(stage, h, buf, landing):
            axis = (h + stage) % 2
            for k in (2, 1, 3):
                group = (coord(axis) + k) % 4
                xy_copy(it, 0, stage, h, k, axis, buf.at[it, h, group], landing.at[it, h, k - 1]).start()

        def total(stage, h, buf, landing):
            part = landing.at[it, h]
            xy_copy(it, 0, stage, h, 1, 0, part, part).wait_recv()
            value = buf[it, h, coord((h + stage) % 2)].astype(F32)
            for k in range(3):
                value = value + landing[it, h, k].astype(F32)
            return value

        for h in range(4):
            send(0, h, zc, r1)
        for h in range(4):
            s2[it, h] = total(0, h, zc, r1).astype(BF16)
            send(1, h, s2, r2)
        pending.append(functools.partial(xy_drain, it, 0, 0, zc.at[it, :, pl.ds(0, 3)]))
        pending.append(functools.partial(xy_drain, it, 0, 1, s2.at[it, :, pl.ds(0, 3)]))
        return [total(1, h, s2, r2) for h in range(4)]

    def three(it, stage, h):
        return bas.at[it, h, 0, pl.ds(0, 3)] if stage == 0 else bas.at[it, h, pl.ds(0, 3)]

    def xy_gather(it, late):
        def block(h, i, j):
            return bas.at[it, h, j, i] if h == 0 else bas.at[it, h, i, j]

        def send(stage, h, ref):
            for k in (2, 1, 3):
                xy_copy(it, 1, stage, h, k, 1 - (h + stage) % 2, ref, ref).start()

        def arrived(stage, h):
            part = three(it, stage, h)
            xy_copy(it, 1, stage, h, 1, 0, part, part).wait_recv()

        place = [(coord(1 - h), coord(h)) for h in (0, 1)]
        for stage in (0, 1):
            for h in (0, 1):
                send(stage, h, block(h, *place[h]))
        late()
        for h in (0, 1):
            arrived(0, h)
            for k in (1, 2, 3):
                send(1, h, block(h, (place[h][0] + k) % 4, place[h][1]))
        for h in (0, 1):
            arrived(1, h)
        for stage in (0, 1):
            pending.append(functools.partial(xy_drain, it, 1, stage, three(it, stage, slice(None))))

    def norm_copy(it, stage, src, dst, k):
        return remote(src, dst, ns.at[it, stage], nr.at[it, stage], norm_dev(stage, k))

    def norm_start(it, stage, value):
        nbuf[it, stage, 0] = jnp.broadcast_to(value, (8, HALF))

        for k in FAR_FIRST[stage]:
            norm_copy(it, stage, nbuf.at[it, stage, 0], nbuf.at[it, stage, k], k).start()
        rest = nbuf.at[it, stage, pl.ds(1, 15)]
        pending.append(norm_copy(it, stage, rest, rest, 1).wait_send)

    def norm_finish(it, stage):
        rest = nbuf.at[it, stage, pl.ds(1, 15)]
        norm_copy(it, stage, rest, rest, 1).wait_recv()
        return jnp.sum(nbuf[it, stage], axis=0)[0:1]

    def scale_of(total):
        return lax.rsqrt(total / TOTAL + 1e-06)

    def give_turn():
        @pl.when(c == 0)
        def _():
            pl.semaphore_signal(turn, inc=1, device_id=partner, device_id_type=pl.DeviceIdType.MESH)

    @pl.when(c == 1)
    def _():
        pl.semaphore_wait(turn, 1)

    lane = lax.broadcasted_iota(jnp.int32, (HALF, BLOCK), 1) < 64

    for it in (0, 1):
        def share_norm():
            if it == 1:
                norm_start(0, 1, norm_finish(0, 0))

        own = z_reduce(it, share_norm)
        pending.append(functools.partial(z_drain, it, 0))
        if it == 1:
            own = own * scale_of(norm_finish(0, 1))
        own = own.astype(BF16)

        yt[it, z] = own.astype(F32).T.astype(BF16)

        def share_image():
            if it == 1:
                ex_i[0] = own[:64]
                ex_i[1] = own[64:]
                remote(ex_i.at[1 - c], ex_i.at[2], es.at[0], er.at[0], partner).start()

        z_gather(it, share_image)
        pending.append(functools.partial(z_drain, it, 1))
        for j in range(BCD):
            blk = slice(j * BLOCK, (j + 1) * BLOCK)
            zero_half = acc[0, :, blk]
            one_half = acc[1, :, blk]
            pair = (
                jnp.where(lane, zero_half, pltpu.roll(one_half, 64, 1)).astype(BF16),
                jnp.where(lane, pltpu.roll(zero_half, 64, 1), one_half).astype(BF16),
            )
            for odd in (0, 1):
                xx, yy = divmod(2 * j + odd, 4)
                for h in range(4):
                    xy = (yy, xx) if h % 2 else (xx, yy)
                    zc[it, h, xy[0], xy[1]] = pair[odd][32 * h : 32 * h + 32]
        second = xy_reduce(it)
        rows = jnp.concatenate(second, axis=0).T
        squares = jnp.sum(rows * rows, axis=0, keepdims=True)
        if it == 0:
            low = rows.astype(BF16)
            bas[1, 0, x, y] = low[:64]
            bas[1, 1, x, y] = low[64:]
            xy_gather(1, functools.partial(norm_start, 0, 0, squares))
        else:
            norm_start(1, 0, squares)
            zfin[...] = rows
            remote(ex_i.at[1 - c], ex_i.at[2], es.at[0], er.at[0], partner).wait()
            image_ref[:, mine] = ex_i[c]
            image_ref[:, theirs] = ex_i[2]
            norm_start(1, 1, norm_finish(1, 0))
            low = (zfin[...] * scale_of(norm_finish(1, 1))).astype(BF16)
            ex_b[0] = low[:64]
            ex_b[1] = low[64:]
            swap = remote(ex_b.at[1 - c], ex_b.at[2], es.at[1], er.at[1], partner)
            swap.start()
            basis_ref[:, mine] = ex_b[c]
            swap.wait()
            basis_ref[:, theirs] = ex_b[2]

    for drain in pending:
        drain()


def shards(block_tiles, block_rows, block_cols, counts, start_basis):
    start = start_basis.reshape(4, 4, 64, 2 * HALF)
    dma = pltpu.SemaphoreType.DMA
    vmem = pltpu.VMEM
    smem = pltpu.SMEM
    scratch = [
        smem((1, NB), jnp.int32), smem((1, NB), jnp.int32), smem((1, 1), jnp.int32),
        smem((1, 128), jnp.int32), smem((1, 128), jnp.int32),
        vmem((1, 128), jnp.int32), vmem((1, 128), jnp.int32),
        vmem((NB + 1, BLOCK, BLOCK), BF16),
        vmem((NB + 1, BLOCK, BLOCK), BF16),
        vmem((2, BRD, BLOCK, 1024), BF16),
        vmem((2, 2, 4, 4, 64, HALF), BF16),
        vmem((2, 15, BLOCK, HALF), BF16),
        vmem((2, 15, BLOCK, HALF), BF16),
        vmem((2, 16, HALF, BLOCK), BF16),
        vmem((2, HALF, 1024), F32),
        vmem((2, 4, 4, 4, 32, BLOCK), BF16),
        vmem((2, 4, 3, 4, 32, BLOCK), BF16),
        vmem((2, 4, 4, 32, BLOCK), BF16),
        vmem((2, 4, 3, 32, BLOCK), BF16),
        vmem((BLOCK, HALF), F32),
        vmem((2, 2, 16, 8, HALF), F32),
        vmem((3, 64, HALF), BF16),
        vmem((3, 64, HALF), BF16),
        dma((3,)), dma((3,)), dma((7,)),
        dma((2, 2)), dma((2, 8)),
        dma((3, 2)), dma((3, 2, 4)),
        dma((2, 2)), dma((2, 2)),
        dma((2,)), dma((2,)),
        pltpu.SemaphoreType.REGULAR,
    ]
    anywhere = pl.BlockSpec(memory_space=pl.ANY)
    in_vmem = pl.BlockSpec(memory_space=pltpu.VMEM)
    return pl.pallas_call(
        kernel,
        out_shape=(
            jax.ShapeDtypeStruct((64, 2 * HALF), BF16),
            jax.ShapeDtypeStruct((64, 2 * HALF), BF16),
        ),
        in_specs=[anywhere] * 5,
        out_specs=(in_vmem, in_vmem),
        scratch_shapes=scratch,
        compiler_params=pltpu.CompilerParams(
            collective_id=0, has_side_effects=True, vmem_limit_bytes=538 * 1024 * 1024 // 10
        ),
    )(block_rows, block_cols, counts, block_tiles, start)


def solution(mesh):
    in_specs = (
        P("row", "col", None, None), P("row", "col"), P("row", "col"), P("row", "col"), P("col", None),
    )
    out_specs = (P(("row", "col"), None), P(("col", "row"), None))
    return jax.shard_map(shards, mesh=mesh, in_specs=in_specs, out_specs=out_specs, check_vma=False)
```

```python
import functools

import jax
import jax.numpy as jnp
from jax import lax
from jax.experimental import pallas as pl
from jax.experimental.pallas import tpu as pltpu
from jax.sharding import PartitionSpec as P

BLOCK = 128
BRD = 16
BCD = 8
NB = 20
HALF = 128
TOTAL = 32768.0
F32 = jnp.float32
BF16 = jnp.bfloat16


TO_OWNER = (5, -5, 3, -3, 2, -2, 1, -1)
RELAYED = (3, 2, 1, -1)

FAR_FIRST = (
    (10, 9, 11, 6, 14, 5, 7, 13, 15, 8, 2, 1, 3, 4, 12),
    (8, 9, 7, 10, 6, 11, 5, 12, 4, 13, 3, 14, 2, 15, 1),
)


def kernel(
    rows_ref, cols_ref, counts_ref, tiles_ref, start_ref, image_ref, basis_ref,
    srows, scols, scount, tab, ptab, tabv, ptabv, tl_own, tl_in, dense, bas, zsnd, zrcv, yt, acc,
    zc, r1, s2, r2, zfin, nbuf, ex_i, ex_b,
    pre_send, pre_recv, loc_sem, zs, zr, xs, xr, ns, nr, es, er, turn,
):
    row = lax.axis_index("row")
    col = lax.axis_index("col")
    x, y = row // 4, row % 4
    z, c = col // 2, col % 2
    sg = 1 - 2 * c

    def at(xx, yy, zz, cc):
        return (((xx + 4) % 4) * 4 + (yy + 4) % 4, ((zz + 16) % 16) * 2 + cc)

    def zpos(e):
        return (z + sg * e + 16) % 16

    def zdev(e):
        return (row, zpos(e) * 2 + c)

    def remote(src, dst, ssem, rsem, dev):
        return pltpu.make_async_remote_copy(
            src_ref=src, dst_ref=dst, send_sem=ssem, recv_sem=rsem,
            device_id=dev, device_id_type=pl.DeviceIdType.MESH,
        )

    partner = (row, z * 2 + 1 - c)
    pending = []

    def norm_dev(stage, k):
        if stage == 0:
            return at(x + k // 4, y + k % 4, z, c)
        return (row, ((z + k) % 16) * 2 + c)

    barrier = pltpu.get_barrier_semaphore()

    def greet(dev):
        pl.semaphore_signal(barrier, inc=1, device_id=dev, device_id_type=pl.DeviceIdType.MESH)

    for k in (3, 2, 1):
        greet(zdev(k))
        greet(zdev(-k))
    for k in (2, 1, 3):
        greet(at(x + k, y, z, c))
        greet(at(x, y + k, z, c))
    greet(partner)

    local = [
        pltpu.make_async_copy(rows_ref, srows, loc_sem.at[0]),
        pltpu.make_async_copy(cols_ref, scols, loc_sem.at[1]),
        pltpu.make_async_copy(counts_ref, scount, loc_sem.at[2]),
        pltpu.make_async_copy(tiles_ref.at[0], tl_own.at[pl.ds(0, NB)], loc_sem.at[3]),
    ]
    for copy in local:
        copy.start()
    mine = pl.ds(pl.multiple_of(c * HALF, HALF), HALF)
    theirs = pl.ds(pl.multiple_of((1 - c) * HALF, HALF), HALF)
    own_start = pltpu.make_async_copy(start_ref.at[:, :, :, mine], bas.at[0, c], loc_sem.at[4])
    own_start.start()
    zero_tile = jnp.zeros((BLOCK, BLOCK), BF16)
    tl_own[NB] = zero_tile
    tl_in[NB] = zero_tile

    for copy in local[:3]:
        copy.wait()
    places = lax.broadcasted_iota(jnp.int32, (1, BRD * BCD), 1)
    slot_of = jnp.full((1, BRD * BCD), NB, jnp.int32)
    for slot in range(NB):
        place = jnp.where(slot < scount[0, 0], srows[0, slot] * BCD + scols[0, slot], -1)
        slot_of = jnp.where(places == place, slot, slot_of)
    tabv[...] = slot_of
    table_own = pltpu.make_async_copy(tabv, tab, loc_sem.at[5])
    table_own.start()

    pl.semaphore_wait(barrier, 13)
    pre = [
        remote(tabv, ptabv, pre_send.at[0], pre_recv.at[0], partner),
        remote(tiles_ref.at[0], tl_in.at[pl.ds(0, NB)], pre_send.at[1], pre_recv.at[1], partner),
        remote(start_ref.at[:, :, :, theirs], bas.at[0, c], pre_send.at[2], pre_recv.at[2], partner),
    ]
    for copy in pre:
        copy.start()

    def build(which, tl, table):
        def one_row(i, carry):
            for j in range(BCD):
                dense[which, i, :, j * BLOCK : (j + 1) * BLOCK] = tl[table[0, i * BCD + j]]
            return carry

        lax.fori_loop(0, BRD, one_row, 0)

    table_own.wait()
    local[3].wait()
    build(c, tl_own, tab)
    pre[0].wait_recv()
    table_in = pltpu.make_async_copy(ptabv, ptab, loc_sem.at[6])
    table_in.start()
    table_in.wait()
    pre[1].wait_recv()
    build(1 - c, tl_in, ptab)
    remote(start_ref.at[:, :, :, theirs], bas.at[0, 1 - c], pre_send.at[2], pre_recv.at[2], partner).wait_recv()
    own_start.wait()
    for copy in pre:
        copy.wait_send()

    def product(it, d):
        left = bas[it, 0].reshape(1024, HALF)
        right = bas[it, 1].reshape(1024, HALF)
        return jnp.dot(dense[0, d], left, preferred_element_type=F32) + jnp.dot(
            dense[1, d], right, preferred_element_type=F32
        )

    def rs_launch(it, m, group, owner, e):
        zsnd[it, m] = product(it, zpos(owner)).astype(BF16)
        rs_send(it, m, group, e)

    def rs_send(it, m, group, e):
        remote(zsnd.at[it, m], zrcv.at[it, m], zs.at[it, 0], zr.at[it, group], zdev(e)).start()

    def rs_arrived(it, group, begin, count):
        part = zrcv.at[it, pl.ds(begin, count)]
        remote(part, part, zs.at[it, 0], zr.at[it, group], zdev(1)).wait_recv()
        return jnp.sum(zrcv[it, begin : begin + count].astype(F32), axis=0)

    def z_reduce(it, late):
        rs_launch(it, 0, 0, 8, 3)

        def outer(k, carry):
            m = 2 * k
            rs_launch(it, m + 1, 0, 7 - k, 2 - k)
            rs_launch(it, m + 5, 1, k - 7, k - 2)
            rs_launch(it, m + 2, 0, 3 + k, k - 2)
            rs_launch(it, m + 6, 1, -3 - k, 2 - k)
            return carry

        lax.fori_loop(0, 2, outer, 0)
        if it == 0:
            give_turn()

        def near(k, carry):
            m = 11 + 2 * k
            rs_launch(it, m, 2, 2 - k, 2 - k)
            rs_launch(it, m + 1, 2, k - 2, k - 2)
            return carry

        lax.fori_loop(0, 2, near, 0)
        ahead = product(it, zpos(5))
        behind = product(it, zpos(-5))
        own = product(it, z)
        late()
        zsnd[it, 9] = (ahead + rs_arrived(it, 0, 0, 5)).astype(BF16)
        rs_send(it, 9, 2, 5)
        zsnd[it, 10] = (behind + rs_arrived(it, 1, 5, 4)).astype(BF16)
        rs_send(it, 10, 2, -5)
        return own + rs_arrived(it, 2, 9, 6)

    def z_drain(it, phase):
        part = (zsnd if phase == 0 else yt).at[it, pl.ds(0, 15)]
        remote(part, part, zs.at[it, phase], zr.at[it, 0], zdev(1)).wait_send()

    def ag_send(it, group, owner, e):
        piece = yt.at[it, zpos(owner)]
        remote(piece, piece, zs.at[it, 1], zr.at[it, group], zdev(e)).start()

    def ag_arrived(it, group, count):
        part = yt.at[it, pl.ds(0, count)]
        remote(part, part, zs.at[it, 1], zr.at[it, group], zdev(1)).wait_recv()

    def add_products(it, pieces, first):
        for which in (0, 1):
            for part in range(2):
                cols = pl.ds(part * 512, 512)
                left = jnp.concatenate([yt[it, zpos(e)] for e in pieces], axis=1)
                right = jnp.concatenate([dense[which, zpos(e), :, cols] for e in pieces], axis=0)
                term = jnp.dot(left, right, preferred_element_type=F32)
                acc[which, :, cols] = term if first else acc[which, :, cols] + term

    def z_gather(it, late):
        for i, e in enumerate(TO_OWNER):
            ag_send(it, 3 + min(i, 2), 0, e)
        late()
        ag_arrived(it, 3, 1)
        for e in RELAYED:
            ag_send(it, 6 if abs(e) == 1 else 7, -5, e)
        ag_arrived(it, 4, 1)
        for e in RELAYED[1:]:
            ag_send(it, 6 if abs(e) == 1 else 7, 5, -e)
        ag_arrived(it, 5, 6)
        add_products(it, [-5, 5, -3, 3, -2, 2, -1, 1, 0], True)
        ag_arrived(it, 6, 4)
        add_products(it, [-6, -4, 4, 6], False)
        ag_arrived(it, 7, 3)
        add_products(it, [-7, 7, -8], False)

    def coord(axis):
        return x if axis == 0 else y

    def axis_dev(axis, k):
        if axis == 0:
            return at(x + k, y, z, c)
        return at(x, y + k, z, c)

    def xy_copy(it, phase, stage, h, k, axis, src, dst):
        p = it * (2 - phase)
        return remote(src, dst, xs.at[p, stage], xr.at[p, stage, h], axis_dev(axis, k))

    def xy_drain(it, phase, stage, part):
        xy_copy(it, phase, stage, 0, 1, 0, part, part).wait_send()

    def xy_reduce(it):
        def send(stage, h, buf, landing):
            axis = (h + stage) % 2
            for k in (2, 1, 3):
                group = (coord(axis) + k) % 4
                xy_copy(it, 0, stage, h, k, axis, buf.at[it, h, group], landing.at[it, h, k - 1]).start()

        def total(stage, h, buf, landing):
            part = landing.at[it, h]
            xy_copy(it, 0, stage, h, 1, 0, part, part).wait_recv()
            value = buf[it, h, coord((h + stage) % 2)].astype(F32)
            for k in range(3):
                value = value + landing[it, h, k].astype(F32)
            return value

        for h in range(4):
            send(0, h, zc, r1)
        for h in range(4):
            s2[it, h] = total(0, h, zc, r1).astype(BF16)
            send(1, h, s2, r2)
        pending.append(functools.partial(xy_drain, it, 0, 0, zc.at[it, :, pl.ds(0, 3)]))
        pending.append(functools.partial(xy_drain, it, 0, 1, s2.at[it, :, pl.ds(0, 3)]))
        return [total(1, h, s2, r2) for h in range(4)]

    def three(it, stage, h):
        return bas.at[it, h, 0, pl.ds(0, 3)] if stage == 0 else bas.at[it, h, pl.ds(0, 3)]

    def xy_gather(it, late):
        def block(h, i, j):
            return bas.at[it, h, j, i] if h == 0 else bas.at[it, h, i, j]

        def send(stage, h, ref):
            for k in (2, 1, 3):
                xy_copy(it, 1, stage, h, k, 1 - (h + stage) % 2, ref, ref).start()

        def arrived(stage, h):
            part = three(it, stage, h)
            xy_copy(it, 1, stage, h, 1, 0, part, part).wait_recv()

        place = [(coord(1 - h), coord(h)) for h in (0, 1)]
        for stage in (0, 1):
            for h in (0, 1):
                send(stage, h, block(h, *place[h]))
        late()
        for h in (0, 1):
            arrived(0, h)
            for k in (1, 2, 3):
                send(1, h, block(h, (place[h][0] + k) % 4, place[h][1]))
        for h in (0, 1):
            arrived(1, h)
        for stage in (0, 1):
            pending.append(functools.partial(xy_drain, it, 1, stage, three(it, stage, slice(None))))

    def norm_copy(it, stage, src, dst, k):
        return remote(src, dst, ns.at[it, stage], nr.at[it, stage], norm_dev(stage, k))

    def norm_start(it, stage, value):
        nbuf[it, stage, 0] = jnp.broadcast_to(value, (8, HALF))

        for k in FAR_FIRST[stage]:
            norm_copy(it, stage, nbuf.at[it, stage, 0], nbuf.at[it, stage, k], k).start()
        rest = nbuf.at[it, stage, pl.ds(1, 15)]
        pending.append(norm_copy(it, stage, rest, rest, 1).wait_send)

    def norm_finish(it, stage):
        rest = nbuf.at[it, stage, pl.ds(1, 15)]
        norm_copy(it, stage, rest, rest, 1).wait_recv()
        return jnp.sum(nbuf[it, stage], axis=0)[0:1]

    def scale_of(total):
        return lax.rsqrt(total / TOTAL + 1e-06)

    def give_turn():
        @pl.when(c == 0)
        def _():
            pl.semaphore_signal(turn, inc=1, device_id=partner, device_id_type=pl.DeviceIdType.MESH)

    @pl.when(c == 1)
    def _():
        pl.semaphore_wait(turn, 1)

    lane = lax.broadcasted_iota(jnp.int32, (HALF, BLOCK), 1) < 64

    for it in (0, 1):
        def share_norm():
            if it == 1:
                norm_start(0, 1, norm_finish(0, 0))

        own = z_reduce(it, share_norm)
        pending.append(functools.partial(z_drain, it, 0))
        if it == 1:
            own = own * scale_of(norm_finish(0, 1))
        own = own.astype(BF16)

        yt[it, z] = own.astype(F32).T.astype(BF16)

        def share_image():
            if it == 1:
                ex_i[0] = own[:64]
                ex_i[1] = own[64:]
                remote(ex_i.at[1 - c], ex_i.at[2], es.at[0], er.at[0], partner).start()

        z_gather(it, share_image)
        pending.append(functools.partial(z_drain, it, 1))
        for j in range(BCD):
            blk = slice(j * BLOCK, (j + 1) * BLOCK)
            zero_half = acc[0, :, blk]
            one_half = acc[1, :, blk]
            pair = (
                jnp.where(lane, zero_half, pltpu.roll(one_half, 64, 1)).astype(BF16),
                jnp.where(lane, pltpu.roll(zero_half, 64, 1), one_half).astype(BF16),
            )
            for odd in (0, 1):
                xx, yy = divmod(2 * j + odd, 4)
                for h in range(4):
                    xy = (yy, xx) if h % 2 else (xx, yy)
                    zc[it, h, xy[0], xy[1]] = pair[odd][32 * h : 32 * h + 32]
        second = xy_reduce(it)
        rows = jnp.concatenate(second, axis=0).T
        squares = jnp.sum(rows * rows, axis=0, keepdims=True)
        if it == 0:
            low = rows.astype(BF16)
            bas[1, 0, x, y] = low[:64]
            bas[1, 1, x, y] = low[64:]
            xy_gather(1, functools.partial(norm_start, 0, 0, squares))
        else:
            norm_start(1, 0, squares)
            zfin[...] = rows
            remote(ex_i.at[1 - c], ex_i.at[2], es.at[0], er.at[0], partner).wait()
            image_ref[:, mine] = ex_i[c]
            image_ref[:, theirs] = ex_i[2]
            norm_start(1, 1, norm_finish(1, 0))
            low = (zfin[...] * scale_of(norm_finish(1, 1))).astype(BF16)
            ex_b[0] = low[:64]
            ex_b[1] = low[64:]
            swap = remote(ex_b.at[1 - c], ex_b.at[2], es.at[1], er.at[1], partner)
            swap.start()
            basis_ref[:, mine] = ex_b[c]
            swap.wait()
            basis_ref[:, theirs] = ex_b[2]

    for drain in pending:
        drain()


def shards(block_tiles, block_rows, block_cols, counts, start_basis):
    start = start_basis.reshape(4, 4, 64, 2 * HALF)
    dma = pltpu.SemaphoreType.DMA
    vmem = pltpu.VMEM
    smem = pltpu.SMEM
    scratch = [
        smem((1, NB), jnp.int32), smem((1, NB), jnp.int32), smem((1, 1), jnp.int32),
        smem((1, 128), jnp.int32), smem((1, 128), jnp.int32),
        vmem((1, 128), jnp.int32), vmem((1, 128), jnp.int32),
        vmem((NB + 1, BLOCK, BLOCK), BF16),
        vmem((NB + 1, BLOCK, BLOCK), BF16),
        vmem((2, BRD, BLOCK, 1024), BF16),
        vmem((2, 2, 4, 4, 64, HALF), BF16),
        vmem((2, 15, BLOCK, HALF), BF16),
        vmem((2, 15, BLOCK, HALF), BF16),
        vmem((2, 16, HALF, BLOCK), BF16),
        vmem((2, HALF, 1024), F32),
        vmem((2, 4, 4, 4, 32, BLOCK), BF16),
        vmem((2, 4, 3, 4, 32, BLOCK), BF16),
        vmem((2, 4, 4, 32, BLOCK), BF16),
        vmem((2, 4, 3, 32, BLOCK), BF16),
        vmem((BLOCK, HALF), F32),
        vmem((2, 2, 16, 8, HALF), F32),
        vmem((3, 64, HALF), BF16),
        vmem((3, 64, HALF), BF16),
        dma((3,)), dma((3,)), dma((7,)),
        dma((2, 2)), dma((2, 8)),
        dma((3, 2)), dma((3, 2, 4)),
        dma((2, 2)), dma((2, 2)),
        dma((2,)), dma((2,)),
        pltpu.SemaphoreType.REGULAR,
    ]
    anywhere = pl.BlockSpec(memory_space=pl.ANY)
    in_vmem = pl.BlockSpec(memory_space=pltpu.VMEM)
    return pl.pallas_call(
        kernel,
        out_shape=(
            jax.ShapeDtypeStruct((64, 2 * HALF), BF16),
            jax.ShapeDtypeStruct((64, 2 * HALF), BF16),
        ),
        in_specs=[anywhere] * 5,
        out_specs=(in_vmem, in_vmem),
        scratch_shapes=scratch,
        compiler_params=pltpu.CompilerParams(
            collective_id=0, has_side_effects=True, vmem_limit_bytes=538 * 1024 * 1024 // 10
        ),
    )(block_rows, block_cols, counts, block_tiles, start)


def solution(mesh):
    in_specs = (
        P("row", "col", None, None), P("row", "col"), P("row", "col"), P("row", "col"), P("col", None),
    )
    out_specs = (P(("row", "col"), None), P(("col", "row"), None))
    return jax.shard_map(shards, mesh=mesh, in_specs=in_specs, out_specs=out_specs, check_vma=False)
```
